32 devices in a mesh: tok: 4 (over y, core), exp: 8 (over z, x).
Axes of the slice: x: 2, y: 2, z: 4, core: 2. Of those that a mesh axis runs over, the one named last changes fastest.
Arguments:
- tokens: bfloat16 [2048, 4096], P(('tok', 'exp')), may hold values from -6 to 6
- cotangent: bfloat16 [2048, 4096], P(('tok', 'exp')), may hold values from -6 to 6
- expert_ids: int32 [2048, 8], P(('tok', 'exp')), may hold values from 0 to 127, as said below
- gate_weights: bfloat16 [2048, 8], P(('tok', 'exp')), may hold values from 0.099609375 to 1
- w_in: bfloat16 [8, 2, 1536, 4096], P('exp', None, 'tok'), may hold values from -0.09375 to 0.09375
- w_down: bfloat16 [8, 1536, 4096], P('exp', 'tok'), may hold values from -0.3125 to 0.3125
Outputs:
- moe_out: bfloat16 [2048, 4096], P(('tok', 'exp'))
- token_grad: bfloat16 [2048, 4096], P(('tok', 'exp'))
- grad_w_in: bfloat16 [8, 2, 1536, 4096], P('exp', None, 'tok')
- grad_w_down: bfloat16 [8, 1536, 4096], P('exp', 'tok')
The draws below stay inside these ranges and needn't reach their ends.
Inputs may be any that keep to these rules, and one draw needn't show every extreme that they name: `expert_ids`: each row names 8 different experts. Among the 64 rows of one device no expert below 8 is named by more than 2 rows, and one expert below 8, the same on every device, is named by exactly 2 rows of every device.
All inputs are finite; a program needn't handle non-finite values.
Results may differ from the reference program's by a relative error of at most 0.0058.
Values may be sent and summed in bfloat16 or wider, within the bound.
No kernel may reach another device: no remote copies, remote signals or barrier semaphores. Data moves between devices by JAX's collectives and lax.ppermute only.
A program may use at most 128 MiB of HBM per device.

```python
import math
import jax
import jax.numpy as jnp
from jax import lax

D = 4096
FF = 1536
EXPERTS_ALL = 128
TOP = 8
TOKENS_PER_CARD = 64
CAP = 2
EXPERTS = 8
TOKENS = 2048


def draw_expert_ids(key, part):
    blocks = TOKENS // TOKENS_PER_CARD
    hot_expert = jax.random.randint(jax.random.fold_in(key, 7), (), 0, EXPERTS).astype(jnp.int32)
    owners = jnp.arange(EXPERTS, dtype=jnp.int32)

    def one_block(block_row):
        block_key = jax.random.fold_in(jax.random.fold_in(key, 11), block_row)
        counts = jax.random.randint(jax.random.fold_in(block_key, 1), (EXPERTS,), 0, CAP + 1).astype(jnp.int32)
        counts = jnp.where(owners == hot_expert, CAP, counts).astype(jnp.int32)
        ranking = jax.random.permutation(jax.random.fold_in(block_key, 2), EXPERTS).astype(jnp.int32)
        row_order = jax.random.permutation(jax.random.fold_in(block_key, 3), TOKENS_PER_CARD).astype(jnp.int32)
        position = jnp.arange(EXPERTS * CAP, dtype=jnp.int32)
        expert_lookup = ranking[position // CAP]
        active_mask = position % CAP < counts[expert_lookup]
        row_lookup = row_order[position]
        pending_rows = jnp.full((TOKENS_PER_CARD,), -1, jnp.int32).at[row_lookup].set(jnp.where(active_mask, expert_lookup, -1).astype(jnp.int32))
        outside = jnp.arange(EXPERTS, EXPERTS_ALL, dtype=jnp.int32)
        table = jnp.broadcast_to(outside[None, :], (TOKENS_PER_CARD, EXPERTS_ALL - EXPERTS))
        remaining_peers = jax.random.permutation(jax.random.fold_in(block_key, 4), table, axis=1, independent=True)[:, :TOP]
        column_slot = jax.random.randint(jax.random.fold_in(block_key, 5), (TOKENS_PER_CARD,), 0, TOP).astype(jnp.int32)
        place_table = jnp.arange(TOP, dtype=jnp.int32)
        substitute_rows = (place_table[None, :] == column_slot[:, None]) & (pending_rows[:, None] >= 0)
        return jnp.where(substitute_rows, pending_rows[:, None], remaining_peers).astype(jnp.int32)
    picks_all = jax.vmap(one_block)(jnp.arange(blocks, dtype=jnp.int32))
    return picks_all.reshape(TOKENS, TOP).astype(jnp.int32)


def block_scale(rng, shape, cuts, low, top_value):
    def one(dim, parts):
        heights = jax.random.uniform(jax.random.fold_in(jax.random.fold_in(rng, 6), dim), (parts,), jnp.float32, low / len(cuts), top_value / len(cuts))
        return jnp.repeat(jnp.exp(heights), shape[dim] // parts).reshape((-1,) + (1,) * (len(shape) - dim - 1))

    gain = one(*cuts[0])
    for cut in cuts[1:]:
        gain = gain * one(*cut)
    return gain


def normal_values(key, shape, deviation, most, split=(), held_as=jnp.bfloat16):
    array = deviation * jax.random.normal(key, shape, jnp.float32)
    if split:
        array = array * block_scale(key, shape, split, -0.22, 0.18)
    return jnp.clip(array, -most, most).astype(held_as)


def setup_inputs(seed: int = 0) -> dict:
    keys = jax.random.split(jax.random.key(seed), 7)
    return {
        "tokens": normal_values(keys[0], (TOKENS, D), 1.0, 6.0, ((0, 32),)),
        "cotangent": normal_values(keys[1], (TOKENS, D), 1.0, 6.0, ((0, 32),)),
        "expert_ids": draw_expert_ids(jax.random.fold_in(keys[6], 71), 0),
        "gate_weights": jnp.clip(jnp.exp(math.log(1.0) - 2.306499 * jax.random.uniform(keys[3], (TOKENS, TOP), jnp.float32) ** block_scale(keys[3], (TOKENS, TOP), ((0, 32),), -0.2, 0.2)), 0.099609375, 1.0).astype(jnp.bfloat16),
        "w_in": normal_values(keys[4], (EXPERTS, 2, FF, D), D ** -0.5, 0.09375, ((0, 8), (2, 4))),
        "w_down": normal_values(keys[5], (EXPERTS, FF, D), (FF // 4) ** -0.5, 0.3125, ((0, 8), (1, 4))),
    }


def expert_pass(operands):
    routed, routed_cot, weight_in, weight_down = operands
    gate_act = jnp.dot(routed, weight_in[0].T, preferred_element_type=jnp.float32)
    up_act = jnp.dot(routed, weight_in[1].T, preferred_element_type=jnp.float32)
    sigmoid_gate = jax.nn.sigmoid(gate_act)
    silu_gate = gate_act * sigmoid_gate
    hidden = (silu_gate * up_act).astype(jnp.bfloat16)
    expert_out = jnp.dot(hidden, weight_down, preferred_element_type=jnp.float32).astype(jnp.bfloat16)
    hidden_grad = jnp.dot(routed_cot, weight_down.T, preferred_element_type=jnp.float32)
    gate_grad = (hidden_grad * up_act * sigmoid_gate * (1.0 + gate_act * (1.0 - sigmoid_gate))).astype(jnp.bfloat16)
    up_grad = (hidden_grad * silu_gate).astype(jnp.bfloat16)
    input_grad = (jnp.dot(gate_grad, weight_in[0], preferred_element_type=jnp.float32)
                  + jnp.dot(up_grad, weight_in[1], preferred_element_type=jnp.float32)).astype(jnp.bfloat16)
    grad_gate = jnp.dot(gate_grad.T, routed, preferred_element_type=jnp.float32).astype(jnp.bfloat16)
    grad_up = jnp.dot(up_grad.T, routed, preferred_element_type=jnp.float32).astype(jnp.bfloat16)
    grad_down = jnp.dot(hidden.T, routed_cot, preferred_element_type=jnp.float32).astype(jnp.bfloat16)
    return expert_out, input_grad, jnp.stack([grad_gate, grad_up]), grad_down


def place_rows(expert_ids):
    blocks = TOKENS // TOKENS_PER_CARD
    flat_ids = expert_ids.reshape(blocks, TOKENS_PER_CARD * TOP).astype(jnp.int32)
    owners = jnp.arange(EXPERTS, dtype=jnp.int32)
    onehot = (flat_ids[:, :, None] == owners[None, None, :]).astype(jnp.int32)
    before = (jnp.cumsum(onehot, axis=1).astype(jnp.int32) - onehot).astype(jnp.int32)
    slots = jnp.sum(before * onehot, axis=2).astype(jnp.int32)
    block_row = jnp.arange(blocks, dtype=jnp.int32)[:, None]
    row_index = flat_ids * (blocks * CAP) + block_row * CAP + slots
    row_index = jnp.where(flat_ids < EXPERTS, row_index, EXPERTS * blocks * CAP).astype(jnp.int32)
    return row_index.reshape(TOKENS, TOP)


def reference(tokens, cotangent, expert_ids, gate_weights, w_in, w_down):
    blocks = TOKENS // TOKENS_PER_CARD
    rows_total = EXPERTS * blocks * CAP
    row_index = place_rows(expert_ids)
    flat_index = row_index.reshape(-1)
    token_of = jnp.broadcast_to(jnp.arange(TOKENS, dtype=jnp.int32)[:, None], (TOKENS, TOP)).reshape(-1)
    source = jnp.full((rows_total,), TOKENS, jnp.int32).at[flat_index].set(token_of, mode="drop")
    gate_rows = jnp.zeros((rows_total,), jnp.float32).at[flat_index].set(
        gate_weights.astype(jnp.float32).reshape(-1), mode="drop")
    padded_tokens = jnp.concatenate([tokens, jnp.zeros((1, D), tokens.dtype)], axis=0)
    padded_cot = jnp.concatenate([cotangent, jnp.zeros((1, D), cotangent.dtype)], axis=0)
    routed = padded_tokens[source]
    routed_cot = (gate_rows[:, None] * padded_cot[source].astype(jnp.float32)).astype(jnp.bfloat16)
    routed = routed.reshape(EXPERTS, blocks * CAP, D)
    routed_cot = routed_cot.reshape(EXPERTS, blocks * CAP, D)
    expert_out, input_grad, grad_w_in, grad_w_down = lax.map(expert_pass, (routed, routed_cot, w_in, w_down))
    out_pad = jnp.concatenate([expert_out.reshape(rows_total, D), jnp.zeros((1, D), jnp.bfloat16)], axis=0)
    grad_pad = jnp.concatenate([input_grad.reshape(rows_total, D), jnp.zeros((1, D), jnp.bfloat16)], axis=0)
    moe_sum = jnp.zeros((TOKENS, D), jnp.float32)
    grad_sum = jnp.zeros((TOKENS, D), jnp.float32)
    for place in range(TOP):
        picked = row_index[:, place]
        moe_sum = moe_sum + gate_weights[:, place].astype(jnp.float32)[:, None] * out_pad[picked].astype(jnp.float32)
        grad_sum = grad_sum + grad_pad[picked].astype(jnp.float32)
    return moe_sum.astype(jnp.bfloat16), grad_sum.astype(jnp.bfloat16), grad_w_in, grad_w_down
```

```python
import functools

import jax
import jax.numpy as jnp
from jax import lax
from jax.experimental import pallas as pl
from jax.experimental.pallas import tpu as pltpu
from jax.sharding import Mesh, PartitionSpec as P

CAP = 2
TILE = 16
CHUNKS = TILE // CAP
PAIR = 2
F32 = jnp.float32
BF16 = jnp.bfloat16
LIMIT = 48 * 1024 * 1024


def iota(shape, dim):
    return lax.broadcasted_iota(jnp.int32, shape, dim)


def dot(a, b, dims=((1,), (0,))):
    return lax.dot_general(a, b, (dims, ((), ())), preferred_element_type=F32)


def vmem():
    return pl.BlockSpec(memory_space=pltpu.VMEM)


def params():
    return pltpu.CompilerParams(vmem_limit_bytes=LIMIT)


def folded(ref, rows, width):
    return jnp.concatenate([ref[0:rows, c * width : (c + 1) * width] for c in range(CHUNKS)], axis=0)


def gather_kernel(ids_ref, gates_ref, tok_ref, cot_ref, send_ref, pick_ref, weigh_ref):
    top, rows = ids_ref.shape
    groups, experts, _, width = send_ref.shape
    ids = ids_ref[...]
    gates = gates_ref[...].astype(F32)
    owner = iota((experts, rows), 0)
    member = jnp.zeros((experts, rows), F32)
    gate = jnp.zeros((experts, rows), F32)
    for k in range(top):
        hit = ids[k : k + 1, :] == owner
        member = member + jnp.where(hit, 1.0, 0.0)
        gate = gate + jnp.where(hit, gates[k : k + 1, :], 0.0)
    earlier = jnp.where(iota((rows, rows), 0) < iota((rows, rows), 1), 1.0, 0.0)
    slot = dot(member.astype(BF16), earlier.astype(BF16))
    picks = jnp.concatenate([jnp.where(slot == c, member, 0.0) for c in range(CAP)], axis=0)
    weights = jnp.concatenate([jnp.where(slot == c, gate, 0.0) for c in range(CAP)], axis=0)
    total = experts * TILE
    line = iota((total, CAP * experts), 0)
    spread = jnp.where(
        iota((total, CAP * experts), 1) == (line % CAP) * experts + line // TILE, 1.0, 0.0
    ).astype(BF16)
    repeat = jnp.where(iota((rows, CHUNKS * rows), 1) % rows == iota((rows, CHUNKS * rows), 0), 1.0, 0.0)
    repeat = repeat.astype(BF16)
    shape = (total, CHUNKS * rows)
    chunk = (iota(shape, 0) // CAP) % CHUNKS == iota(shape, 1) // rows
    for part, (table, source, out) in enumerate(
        ((picks, tok_ref, pick_ref), (weights, cot_ref, weigh_ref))
    ):
        small = dot(spread, table.astype(BF16)).astype(BF16)
        wide = jnp.where(chunk, dot(small, repeat), 0.0).astype(BF16)
        out[...] = wide
        moved = dot(wide, folded(source, rows, width)).astype(BF16).reshape(experts, TILE, width)
        for g in range(groups):
            send_ref[g, :, part * TILE : (part + 1) * TILE, :] = moved


def expert_kernel(
    near_ref, far_ref, w_in_ref, w_down_ref,
    keep_ref, away_ref, x_ref, c_ref, hid_ref, gg_ref, ug_ref,
):
    sources, _, width = near_ref.shape
    half = sources * CAP
    lines = sources * TILE
    row, col = iota((lines, lines), 0), iota((lines, lines), 1)
    perm = (row % half // CAP) * TILE + (row // half) * CAP + row % CAP == col
    perm = jnp.where(perm, 1.0, 0.0).astype(BF16)
    for side, ref in enumerate((near_ref, far_ref)):
        for part, out in enumerate((x_ref, c_ref)):
            flat = ref[:, part * TILE : (part + 1) * TILE, :].reshape(lines, width)
            flat = dot(perm, flat).astype(BF16)
            for c in range(CHUNKS):
                out[side * half : (side + 1) * half, c * width : (c + 1) * width] = flat[
                    c * half : (c + 1) * half
                ]
    x = x_ref[...]
    gate = dot(w_in_ref[0], x, ((1,), (1,)))
    up = dot(w_in_ref[1], x, ((1,), (1,)))
    sig = jax.nn.sigmoid(gate)
    silu = gate * sig
    hid = silu * up
    hid_ref[...] = hid.astype(BF16)
    grad = dot(w_down_ref[...], c_ref[...], ((1,), (1,)))
    gg = grad * up * sig * (1.0 + gate * (1.0 - sig))
    ug = grad * silu
    gg_ref[...] = gg.astype(BF16)
    ug_ref[...] = ug.astype(BF16)
    hid_rows = hid.T.astype(BF16)
    gg_rows = gg.T.astype(BF16)
    ug_rows = ug.T.astype(BF16)
    for c in range(CHUNKS):
        cols = pl.ds(c * width, width)
        out = dot(hid_rows, w_down_ref[:, cols])
        back = dot(gg_rows, w_in_ref[0, :, cols]) + dot(ug_rows, w_in_ref[1, :, cols])
        keep_ref[0, :, cols] = out[:half]
        keep_ref[1, :, cols] = back[:half]
        away_ref[0, :, cols] = out[half:].astype(BF16)
        away_ref[1, :, cols] = back[half:].astype(BF16)


def merge_kernel(keep_ref, other_ref, send_ref):
    sources, _, width = send_ref.shape
    half = sources * CAP
    lines = sources * TILE
    row, col = iota((lines, lines), 0), iota((lines, lines), 1)
    perm = (row // CAP % CHUNKS) * half + (row // TILE) * CAP + row % CAP == col
    perm = jnp.where(perm, 1.0, 0.0).astype(BF16)
    for part in range(2):
        pieces = []
        for c in range(CHUNKS):
            cols = pl.ds(c * width, width)
            pieces.append((keep_ref[part, :, cols] + other_ref[part, :, cols].astype(F32)).astype(BF16))
        flat = dot(perm, jnp.concatenate(pieces, axis=0)).astype(BF16)
        send_ref[:, part * TILE : (part + 1) * TILE, :] = flat.reshape(sources, TILE, width)


def weight_kernel(x_ref, c_ref, hid_ref, gg_ref, ug_ref, win_ref, wdown_ref):
    x = x_ref[...]
    win_ref[0] = dot(gg_ref[...], x).astype(BF16)
    win_ref[1] = dot(ug_ref[...], x).astype(BF16)
    wdown_ref[...] = dot(hid_ref[...], c_ref[...]).astype(BF16)


def combine_kernel(back_ref, pick_ref, weigh_ref, moe_ref, grad_ref):
    groups, experts, _, width = back_ref.shape
    rows = moe_ref.shape[0]
    for part, (table, out) in enumerate(((weigh_ref, moe_ref), (pick_ref, grad_ref))):
        total = back_ref[0, :, part * TILE : (part + 1) * TILE, :].astype(F32)
        for g in range(1, groups):
            total = total + back_ref[g, :, part * TILE : (part + 1) * TILE, :].astype(F32)
        flat = total.astype(BF16).reshape(experts * TILE, width)
        wide = dot(table[...], flat, ((0,), (0,))).astype(BF16)
        for c in range(CHUNKS):
            out[:, c * width : (c + 1) * width] = wide[c * rows : (c + 1) * rows]


def body(tokens, cotangent, expert_ids, gate_weights, w_in, w_down):
    groups, experts = lax.axis_size("row"), lax.axis_size("exp")
    rows, depth = tokens.shape
    width = depth // CHUNKS
    sources = groups * experts
    hidden = w_down.shape[1]
    w_in, w_down = w_in[0], w_down[0]
    table = jax.ShapeDtypeStruct((experts * TILE, CHUNKS * rows), BF16)
    send, pick, weigh = pl.pallas_call(
        gather_kernel,
        out_shape=(jax.ShapeDtypeStruct((groups, experts, 2 * TILE, width), BF16), table, table),
        in_specs=[vmem()] * 4,
        out_specs=[vmem()] * 3,
        compiler_params=params(),
        name="gather_rows",
    )(expert_ids.T, gate_weights.T, tokens, cotangent)

    def exchange(array):
        return lax.all_to_all(array, ("row", "exp"), split_axis=0, concat_axis=0, tiled=True)

    def swap(array):
        return lax.ppermute(array, "pair", [(i, PAIR - 1 - i) for i in range(PAIR)])

    near = exchange(send.reshape(sources, 2 * TILE, width))
    far = swap(near)
    half = sources * CAP
    wide = jax.ShapeDtypeStruct((2 * half, depth), BF16)
    tall = jax.ShapeDtypeStruct((hidden, 2 * half), BF16)
    keep, away, x, c, hid, gg, ug = pl.pallas_call(
        expert_kernel,
        out_shape=(
            jax.ShapeDtypeStruct((2, half, depth), F32),
            jax.ShapeDtypeStruct((2, half, depth), BF16),
            wide, wide, tall, tall, tall,
        ),
        in_specs=[vmem()] * 4,
        out_specs=[vmem()] * 7,
        compiler_params=params(),
        name="expert_rows",
    )(near, far, w_in, w_down)
    other = swap(away)
    merged = pl.pallas_call(
        merge_kernel,
        out_shape=jax.ShapeDtypeStruct((sources, 2 * TILE, width), BF16),
        in_specs=[vmem()] * 2,
        out_specs=vmem(),
        compiler_params=params(),
        name="merge_pair",
    )(keep, other)
    back = exchange(merged).reshape(groups, experts, 2 * TILE, width)
    flops = 2 * 3 * hidden * depth * 2 * half
    grad_in, grad_down = pl.pallas_call(
        weight_kernel,
        grid=(CHUNKS,),
        out_shape=(
            jax.ShapeDtypeStruct((2, hidden, depth), BF16),
            jax.ShapeDtypeStruct((hidden, depth), BF16),
        ),
        in_specs=[
            pl.BlockSpec((2 * half, width), lambda i: (0, i)),
            pl.BlockSpec((2 * half, width), lambda i: (0, i)),
        ]
        + [pl.BlockSpec((hidden, 2 * half), lambda i: (0, 0))] * 3,
        out_specs=(
            pl.BlockSpec((2, hidden, width), lambda i: (0, 0, i)),
            pl.BlockSpec((hidden, width), lambda i: (0, i)),
        ),
        compiler_params=params(),
        cost_estimate=pl.CostEstimate(
            flops=flops, bytes_accessed=3 * hidden * depth * 2 + 4 * half * depth, transcendentals=0
        ),
        name="weight_grads",
    )(x, c, hid, gg, ug)
    moe_out, token_grad = pl.pallas_call(
        combine_kernel,
        out_shape=(jax.ShapeDtypeStruct((rows, depth), BF16),) * 2,
        in_specs=[vmem()] * 3,
        out_specs=[vmem()] * 2,
        compiler_params=params(),
        name="combine_rows",
    )(back, pick, weigh)
    return (moe_out, token_grad, grad_in[None], grad_down[None])


def solution(mesh):
    tok, exp = mesh.shape["tok"], mesh.shape["exp"]
    fine = Mesh(mesh.devices.reshape(tok // PAIR, PAIR, exp), ("row", "pair", "exp"))
    rows = P(("row", "pair", "exp"), None)
    win, wdown = P("exp", None, ("row", "pair"), None), P("exp", ("row", "pair"), None)
    return jax.shard_map(
        body,
        mesh=fine,
        in_specs=(rows, rows, rows, rows, win, wdown),
        out_specs=(rows, rows, win, wdown),
        check_vma=False,
    )
```

```python
import functools

import jax
import jax.numpy as jnp
from jax import lax
from jax.experimental import pallas as pl
from jax.experimental.pallas import tpu as pltpu
from jax.sharding import Mesh, PartitionSpec as P

CAP = 2
TILE = 16
CHUNKS = TILE // CAP
PAIR = 2
F32 = jnp.float32
BF16 = jnp.bfloat16
LIMIT = 24 * 1024 * 1024


def iota(shape, dim):
    return lax.broadcasted_iota(jnp.int32, shape, dim)


def dot(a, b, dims=((1,), (0,))):
    return lax.dot_general(a, b, (dims, ((), ())), preferred_element_type=F32)


def vmem():
    return pl.BlockSpec(memory_space=pltpu.VMEM)


def hbm():
    return pl.BlockSpec(memory_space=pltpu.HBM)


def in_hbm(array):
    return pltpu.with_memory_space_constraint(array, pltpu.HBM)


def params():
    return pltpu.CompilerParams(vmem_limit_bytes=LIMIT)


def folded(ref, rows, width):
    return jnp.concatenate([ref[0:rows, c * width : (c + 1) * width] for c in range(CHUNKS)], axis=0)


def slot_tables(ids, gates, experts):
    top, rows = ids.shape
    gates = gates.astype(F32)
    owner = iota((experts, rows), 0)
    member = jnp.zeros((experts, rows), F32)
    gate = jnp.zeros((experts, rows), F32)
    for k in range(top):
        hit = ids[k : k + 1, :] == owner
        member = member + jnp.where(hit, 1.0, 0.0)
        gate = gate + jnp.where(hit, gates[k : k + 1, :], 0.0)
    earlier = jnp.where(iota((rows, rows), 0) < iota((rows, rows), 1), 1.0, 0.0)
    slot = dot(member.astype(BF16), earlier.astype(BF16))
    picks = jnp.concatenate([jnp.where(slot == c, member, 0.0) for c in range(CAP)], axis=0)
    weights = jnp.concatenate([jnp.where(slot == c, gate, 0.0) for c in range(CAP)], axis=0)
    return picks.astype(BF16), weights.astype(BF16)


def message_masks(experts, rows):
    total = experts * TILE
    line = iota((total, CAP * experts), 0)
    spread = iota((total, CAP * experts), 1) == (line % CAP) * experts + line // TILE
    repeat = iota((rows, CHUNKS * rows), 1) % rows == iota((rows, CHUNKS * rows), 0)
    shape = (total, CHUNKS * rows)
    chunk = (iota(shape, 0) // CAP) % CHUNKS == iota(shape, 1) // rows
    return jnp.where(spread, 1.0, 0.0).astype(BF16), jnp.where(repeat, 1.0, 0.0).astype(BF16), chunk


def widen(table, masks):
    spread, repeat, chunk = masks
    small = dot(spread, table).astype(BF16)
    return jnp.where(chunk, dot(small, repeat), 0.0).astype(BF16)


def gather_kernel(
    ids_hbm, gates_hbm, tok_hbm, cot_hbm,
    send_ref,
    ids_ref, gates_ref, tok_ref, cot_ref, sems,
):
    pairs = ((ids_hbm, ids_ref), (gates_hbm, gates_ref), (tok_hbm, tok_ref), (cot_hbm, cot_ref))
    copies = [pltpu.make_async_copy(a, b, sems.at[i]) for i, (a, b) in enumerate(pairs)]
    for copy in copies:
        copy.start()
    rows = ids_ref.shape[1]
    groups, experts, _, width = send_ref.shape
    masks = message_masks(experts, rows)
    copies[0].wait()
    copies[1].wait()
    tables = slot_tables(ids_ref[...], gates_ref[...], experts)
    wide = [widen(table, masks) for table in tables]
    for part, source in enumerate((tok_ref, cot_ref)):
        copies[2 + part].wait()
        moved = dot(wide[part], folded(source, rows, width)).astype(BF16)
        moved = moved.reshape(experts, TILE, width)
        for g in range(groups):
            send_ref[g, :, part * TILE : (part + 1) * TILE, :] = moved


def table_kernel(ids_ref, gates_ref, after_ref, pick_ref, weigh_ref):
    del after_ref
    rows = ids_ref.shape[1]
    experts = pick_ref.shape[0] // TILE
    masks = message_masks(experts, rows)
    picks, weights = slot_tables(ids_ref[...], gates_ref[...], experts)
    pick_ref[...] = widen(picks, masks)
    weigh_ref[...] = widen(weights, masks)


def unfold(ref, part, perm, out):
    sources, _, width = ref.shape
    half = sources * CAP
    flat = ref[:, part * TILE : (part + 1) * TILE, :].reshape(sources * TILE, width)
    flat = dot(perm, flat).astype(BF16)
    for c in range(CHUNKS):
        out[:, c * width : (c + 1) * width] = flat[c * half : (c + 1) * half]


def unfold_table(sources):
    half, lines = sources * CAP, sources * TILE
    row, col = iota((lines, lines), 0), iota((lines, lines), 1)
    perm = (row % half // CAP) * TILE + (row // half) * CAP + row % CAP == col
    return jnp.where(perm, 1.0, 0.0).astype(BF16)


def near_kernel(near_ref, w_in_hbm, w_down_hbm, w_in_ref, w_down_ref, x_ref, c_ref, sems):
    hidden = w_down_hbm.shape[0]
    part = hidden // 2
    copies = []
    for source, target in (
        (w_in_hbm.at[0], w_in_ref.at[0]),
        (w_in_hbm.at[1], w_in_ref.at[1]),
        (w_down_hbm, w_down_ref),
    ):
        for low in (0, part):
            copies.append(
                pltpu.make_async_copy(
                    source.at[low : low + part], target.at[low : low + part], sems.at[len(copies)]
                )
            )
            copies[-1].start()
    perm = unfold_table(near_ref.shape[0])
    unfold(near_ref, 0, perm, x_ref)
    unfold(near_ref, 1, perm, c_ref)
    for copy in copies:
        copy.wait()


def expert_kernel(
    far_ref, x_near, c_near, w_in_ref, w_down_ref,
    keep_ref, away_ref, x_ref, c_ref, hid_ref, gg_ref, ug_ref,
):
    sources, _, width = far_ref.shape
    half = sources * CAP
    hidden = w_down_ref.shape[0]
    perm = unfold_table(sources)
    x_ref[0:half, :] = x_near[...]
    unfold(far_ref, 0, perm, x_ref.at[half : 2 * half])
    c_ref[0:half, :] = c_near[...]
    unfold(far_ref, 1, perm, c_ref.at[half : 2 * half])
    last = ((1,), (1,))
    both = dot(w_in_ref[...].reshape(2 * hidden, -1), x_ref[...], last)
    grad = dot(w_down_ref[...], c_ref[...], last)
    gate, up = both[:hidden], both[hidden:]
    sig = jax.nn.sigmoid(gate)
    silu = gate * sig
    hid = silu * up
    gg = grad * up * sig * (1.0 + gate * (1.0 - sig))
    ug = grad * silu
    hid_ref[...] = hid.astype(BF16)
    gg_ref[...] = gg.astype(BF16)
    ug_ref[...] = ug.astype(BF16)
    hid_rows = hid.T.astype(BF16)
    grad_rows = jnp.concatenate([gg.T, ug.T], axis=1).astype(BF16)
    for c in range(CHUNKS):
        cols = pl.ds(c * width, width)
        out = dot(hid_rows, w_down_ref[:, cols])
        back = dot(grad_rows, w_in_ref[:, :, cols].reshape(2 * hidden, width))
        keep_ref[0, :, cols] = out[:half]
        keep_ref[1, :, cols] = back[:half]
        away_ref[0, :, cols] = out[half:].astype(BF16)
        away_ref[1, :, cols] = back[half:].astype(BF16)


def merge_kernel(keep_ref, other_ref, send_ref):
    sources, _, width = send_ref.shape
    half = sources * CAP
    lines = sources * TILE
    row, col = iota((lines, lines), 0), iota((lines, lines), 1)
    perm = (row // CAP % CHUNKS) * half + (row // TILE) * CAP + row % CAP == col
    perm = jnp.where(perm, 1.0, 0.0).astype(BF16)
    for part in range(2):
        pieces = []
        for c in range(CHUNKS):
            cols = pl.ds(c * width, width)
            pieces.append((keep_ref[part, :, cols] + other_ref[part, :, cols].astype(F32)).astype(BF16))
        flat = dot(perm, jnp.concatenate(pieces, axis=0)).astype(BF16)
        send_ref[:, part * TILE : (part + 1) * TILE, :] = flat.reshape(sources, TILE, width)


def weight_kernel(x_ref, c_ref, hid_ref, gg_ref, ug_ref, win_ref, wdown_ref):
    x = x_ref[...]
    win_ref[0] = dot(gg_ref[...], x).astype(BF16)
    win_ref[1] = dot(ug_ref[...], x).astype(BF16)
    wdown_ref[...] = dot(hid_ref[...], c_ref[...]).astype(BF16)


def combine_kernel(back_ref, pick_ref, weigh_ref, moe_hbm, grad_hbm, moe_ref, grad_ref, sems):
    groups, experts, _, width = back_ref.shape
    rows = moe_ref.shape[0]
    copies = []
    for part, (table, out, home) in enumerate(
        ((weigh_ref, moe_ref, moe_hbm), (pick_ref, grad_ref, grad_hbm))
    ):
        total = back_ref[0, :, part * TILE : (part + 1) * TILE, :].astype(F32)
        for g in range(1, groups):
            total = total + back_ref[g, :, part * TILE : (part + 1) * TILE, :].astype(F32)
        flat = total.astype(BF16).reshape(experts * TILE, width)
        wide = dot(table[...], flat, ((0,), (0,))).astype(BF16)
        for c in range(CHUNKS):
            out[:, c * width : (c + 1) * width] = wide[c * rows : (c + 1) * rows]
        copies.append(pltpu.make_async_copy(out, home, sems.at[part]))
        copies[-1].start()
    for copy in copies:
        copy.wait()


def body(tokens, cotangent, expert_ids, gate_weights, w_in, w_down):
    groups, experts = lax.axis_size("row"), lax.axis_size("exp")
    rows, depth = tokens.shape
    width = depth // CHUNKS
    sources = groups * experts
    hidden = w_down.shape[1]
    w_in, w_down = in_hbm(w_in[0]), in_hbm(w_down[0])
    ids, gates = expert_ids.T, gate_weights.T
    send = pl.pallas_call(
        gather_kernel,
        out_shape=pltpu.VMEM((groups, experts, 2 * TILE, width), BF16),
        in_specs=[hbm()] * 4,
        out_specs=vmem(),
        scratch_shapes=[
            pltpu.VMEM(ids.shape, ids.dtype),
            pltpu.VMEM(gates.shape, gates.dtype),
            pltpu.VMEM(tokens.shape, tokens.dtype),
            pltpu.VMEM(cotangent.shape, cotangent.dtype),
            pltpu.SemaphoreType.DMA((4,)),
        ],
        compiler_params=params(),
        name="gather_rows",
    )(in_hbm(ids), in_hbm(gates), in_hbm(tokens), in_hbm(cotangent))

    def exchange(array):
        return lax.all_to_all(array, ("row", "exp"), split_axis=0, concat_axis=0, tiled=True)

    def swap(array):
        return lax.ppermute(array, "pair", [(i, PAIR - 1 - i) for i in range(PAIR)])

    near = exchange(send.reshape(sources, 2 * TILE, width))
    far = swap(near)
    half = sources * CAP
    w_in, w_down, x_near, c_near = pl.pallas_call(
        near_kernel,
        out_shape=(pltpu.VMEM(w_in.shape, BF16), pltpu.VMEM(w_down.shape, BF16))
        + (pltpu.VMEM((half, depth), BF16),) * 2,
        in_specs=[vmem(), hbm(), hbm()],
        out_specs=[vmem()] * 4,
        scratch_shapes=[pltpu.SemaphoreType.DMA((6,))],
        compiler_params=params(),
        cost_estimate=pl.CostEstimate(flops=0, bytes_accessed=2 * (w_in.size + w_down.size), transcendentals=0),
        name="near_rows",
    )(near, w_in, w_down)
    wide, tall = (2 * half, depth), (hidden, 2 * half)
    keep, away, x, c, hid, gg, ug = pl.pallas_call(
        expert_kernel,
        out_shape=[pltpu.VMEM((2, half, depth), F32), pltpu.VMEM((2, half, depth), BF16)]
        + [jax.ShapeDtypeStruct(shape, BF16) for shape in (wide, wide, tall, tall, tall)],
        in_specs=[vmem()] * 5,
        out_specs=[vmem()] * 7,
        compiler_params=params(),
        name="expert_rows",
    )(far, x_near, c_near, w_in, w_down)
    other = swap(away)
    merged = pl.pallas_call(
        merge_kernel,
        out_shape=pltpu.VMEM((sources, 2 * TILE, width), BF16),
        in_specs=[vmem()] * 2,
        out_specs=vmem(),
        compiler_params=params(),
        name="merge_pair",
    )(keep, other)
    back = exchange(merged).reshape(groups, experts, 2 * TILE, width)
    flops = 2 * 3 * hidden * depth * 2 * half
    grad_in, grad_down = pl.pallas_call(
        weight_kernel,
        grid=(CHUNKS,),
        out_shape=(
            jax.ShapeDtypeStruct((2, hidden, depth), BF16),
            jax.ShapeDtypeStruct((hidden, depth), BF16),
        ),
        in_specs=[
            pl.BlockSpec((2 * half, width), lambda i: (0, i)),
            pl.BlockSpec((2 * half, width), lambda i: (0, i)),
        ]
        + [pl.BlockSpec((hidden, 2 * half), lambda i: (0, 0))] * 3,
        out_specs=(
            pl.BlockSpec((2, hidden, width), lambda i: (0, 0, i)),
            pl.BlockSpec((hidden, width), lambda i: (0, i)),
        ),
        compiler_params=params(),
        cost_estimate=pl.CostEstimate(
            flops=flops, bytes_accessed=3 * hidden * depth * 2 + 4 * half * depth, transcendentals=0
        ),
        name="weight_grads",
    )(x, c, hid, gg, ug)
    table = pltpu.VMEM((experts * TILE, CHUNKS * rows), BF16)
    pick, weigh = pl.pallas_call(
        table_kernel,
        out_shape=(table, table),
        in_specs=[vmem(), vmem(), pl.BlockSpec(memory_space=pl.ANY)],
        out_specs=[vmem()] * 2,
        compiler_params=params(),
        name="slot_tables",
    )(ids, gates, gg)
    moe_out, token_grad = pl.pallas_call(
        combine_kernel,
        out_shape=(pltpu.HBM((rows, depth), BF16),) * 2,
        in_specs=[vmem()] * 3,
        out_specs=[hbm()] * 2,
        scratch_shapes=[pltpu.VMEM((rows, depth), BF16)] * 2 + [pltpu.SemaphoreType.DMA((2,))],
        compiler_params=params(),
        name="combine_rows",
    )(back, pick, weigh)
    return (moe_out, token_grad, grad_in[None], grad_down[None])


def solution(mesh):
    tok, exp = mesh.shape["tok"], mesh.shape["exp"]
    fine = Mesh(mesh.devices.reshape(tok // PAIR, PAIR, exp), ("row", "pair", "exp"))
    rows = P(("row", "pair", "exp"), None)
    win, wdown = P("exp", None, ("row", "pair"), None), P("exp", ("row", "pair"), None)
    return jax.shard_map(
        body,
        mesh=fine,
        in_specs=(rows, rows, rows, rows, win, wdown),
        out_specs=(rows, rows, win, wdown),
        check_vma=False,
    )
```

```python
import functools

import jax
import jax.numpy as jnp
import numpy as np
from jax import lax
from jax.experimental import pallas as pl
from jax.experimental.pallas import tpu as pltpu
from jax.sharding import Mesh, PartitionSpec as P

CAP = 2
TILE = 16
CHUNKS = TILE // CAP
PAIR = 2
STEPS = 2
ORDER_SEED = 2
F32 = jnp.float32
BF16 = jnp.bfloat16
LIMIT = 24 * 1024 * 1024


def iota(shape, dim):
    return lax.broadcasted_iota(jnp.int32, shape, dim)


def dot(a, b, dims=((1,), (0,))):
    return lax.dot_general(a, b, (dims, ((), ())), preferred_element_type=F32)


def vmem():
    return pl.BlockSpec(memory_space=pltpu.VMEM)


def hbm():
    return pl.BlockSpec(memory_space=pltpu.HBM)


def in_hbm(array):
    return pltpu.with_memory_space_constraint(array, pltpu.HBM)


def params():
    return pltpu.CompilerParams(vmem_limit_bytes=LIMIT)


def cost(flops, moved):
    return pl.CostEstimate(flops=flops, bytes_accessed=moved, transcendentals=0)


def slot_tables(ids, gates, experts):
    top, rows = ids.shape
    gates = gates.astype(F32)
    owner = iota((experts, rows), 0)
    member = jnp.zeros((experts, rows), F32)
    gate = jnp.zeros((experts, rows), F32)
    for k in range(top):
        hit = ids[k : k + 1, :] == owner
        member = member + jnp.where(hit, 1.0, 0.0)
        gate = gate + jnp.where(hit, gates[k : k + 1, :], 0.0)
    earlier = jnp.where(iota((rows, rows), 0) < iota((rows, rows), 1), 1.0, 0.0)
    slot = dot(member.astype(BF16), earlier.astype(BF16))
    picks = jnp.concatenate([jnp.where(slot == c, member, 0.0) for c in range(CAP)], axis=0)
    weights = jnp.concatenate([jnp.where(slot == c, gate, 0.0) for c in range(CAP)], axis=0)
    return picks.astype(BF16), weights.astype(BF16)


def message_masks(experts, rows):
    total = experts * TILE
    line = iota((total, CAP * experts), 0)
    spread = iota((total, CAP * experts), 1) == (line % CAP) * experts + line // TILE
    repeat = iota((rows, CHUNKS * rows), 1) % rows == iota((rows, CHUNKS * rows), 0)
    shape = (total, CHUNKS * rows)
    chunk = (iota(shape, 0) // CAP) % CHUNKS == iota(shape, 1) // rows
    return jnp.where(spread, 1.0, 0.0).astype(BF16), jnp.where(repeat, 1.0, 0.0).astype(BF16), chunk


def widen(table, masks):
    spread, repeat, chunk = masks
    small = dot(spread, table).astype(BF16)
    return jnp.where(chunk, dot(small, repeat), 0.0).astype(BF16)


def gather_kernel(
    owners, ids_hbm, gates_hbm, tok_hbm, cot_hbm,
    send_ref,
    ids_ref, gates_ref, tok_ref, cot_ref, sems,
):
    rows, depth = tok_ref.shape
    width = depth // CHUNKS
    experts = max(owners) + 1
    pairs = ((ids_hbm, ids_ref), (gates_hbm, gates_ref), (tok_hbm, tok_ref), (cot_hbm, cot_ref))
    copies = [pltpu.make_async_copy(a, b, sems.at[i]) for i, (a, b) in enumerate(pairs)]
    for copy in copies:
        copy.start()
    masks = message_masks(experts, rows)
    copies[0].wait()
    copies[1].wait()
    tables = slot_tables(ids_ref[...], gates_ref[...], experts)
    wide = [widen(table, masks) for table in tables]
    for part, source in enumerate((tok_ref, cot_ref)):
        copies[2 + part].wait()
        folded = jnp.concatenate(
            [source[:, c * width : (c + 1) * width] for c in range(CHUNKS)], axis=0
        )
        moved = dot(wide[part], folded).astype(BF16).reshape(experts, TILE, width)
        for place, owner in enumerate(owners):
            send_ref[place, part * TILE : (part + 1) * TILE, :] = moved[owner]


def table_kernel(ids_ref, gates_ref, after_ref, pick_ref, weigh_ref):
    del after_ref
    rows = ids_ref.shape[1]
    experts = pick_ref.shape[1] // TILE
    masks = message_masks(experts, rows)
    picks, weights = slot_tables(ids_ref[...], gates_ref[...], experts)
    pick_ref[...] = widen(picks, masks).T
    weigh_ref[...] = widen(weights, masks).T


def unfold(ref, part, perm, out):
    sources, _, width = ref.shape
    half = sources * CAP
    flat = ref[:, part * TILE : (part + 1) * TILE, :].reshape(sources * TILE, width)
    flat = dot(perm, flat).astype(BF16)
    for c in range(CHUNKS):
        out[:, c * width : (c + 1) * width] = flat[c * half : (c + 1) * half]


def near_kernel(near_ref, w_in_hbm, w_in_ref, x_ref, c_ref, unfold_ref, fold_ref, sem):
    fetch = pltpu.make_async_copy(w_in_hbm, w_in_ref, sem)
    fetch.start()
    sources = near_ref.shape[0]
    half, lines = sources * CAP, sources * TILE
    row, col = iota((lines, lines), 0), iota((lines, lines), 1)
    perm = (row % half // CAP) * TILE + (row // half) * CAP + row % CAP == col
    perm = jnp.where(perm, 1.0, 0.0).astype(BF16)
    unfold_ref[...] = perm
    back = (row // CAP % CHUNKS) * half + (row // TILE) * CAP + row % CAP == col
    fold_ref[...] = jnp.where(back, 1.0, 0.0).astype(BF16)
    unfold(near_ref, 0, perm, x_ref)
    unfold(near_ref, 1, perm, c_ref)
    fetch.wait()


def forward_kernel(
    far_ref, x_near, unfold_ref, w_in_ref, w_down_hbm,
    x_ref, hid_ref, gate_slope_ref, up_slope_ref, w_down_ref, sem,
):
    fetch = pltpu.make_async_copy(w_down_hbm, w_down_ref, sem)
    fetch.start()
    hidden = w_down_ref.shape[0]
    half = far_ref.shape[0] * CAP
    x_ref[0:half, :] = x_near[...]
    unfold(far_ref, 0, unfold_ref[...], x_ref.at[half : 2 * half])
    both = dot(w_in_ref[...].reshape(2 * hidden, -1), x_ref[...], ((1,), (1,)))
    gate, up = both[:hidden], both[hidden:]
    sig = jax.nn.sigmoid(gate)
    silu = gate * sig
    hid_ref[...] = (silu * up).astype(BF16)
    gate_slope_ref[...] = up * sig * (1.0 + gate * (1.0 - sig))
    up_slope_ref[...] = silu
    fetch.wait()


def split_rows(value, cols, keep_ref, away_ref):
    half = keep_ref.shape[0]
    keep_ref[:, cols] = value[:half]
    away_ref[:, cols] = value[half:].astype(BF16)


def down_kernel(hid_ref, w_down_ref, keep_ref, away_ref):
    width = w_down_ref.shape[1] // CHUNKS
    rows = hid_ref[...].T
    for c in range(CHUNKS):
        cols = pl.ds(c * width, width)
        split_rows(dot(rows, w_down_ref[:, cols]), cols, keep_ref, away_ref)


def hidden_kernel(
    far_ref, c_near, unfold_ref, w_down_ref, gate_slope_ref, up_slope_ref, c_ref, gg_ref, ug_ref
):
    half = far_ref.shape[0] * CAP
    c_ref[0:half, :] = c_near[...]
    unfold(far_ref, 1, unfold_ref[...], c_ref.at[half : 2 * half])
    grad = dot(w_down_ref[...], c_ref[...], ((1,), (1,)))
    gg_ref[...] = (grad * gate_slope_ref[...]).astype(BF16)
    ug_ref[...] = (grad * up_slope_ref[...]).astype(BF16)


def back_kernel(gg_ref, ug_ref, w_in_ref, keep_ref, away_ref):
    width = w_in_ref.shape[2] // CHUNKS
    gate_rows, up_rows = gg_ref[...].T, ug_ref[...].T
    for c in range(CHUNKS):
        cols = pl.ds(c * width, width)
        value = dot(gate_rows, w_in_ref[0, :, cols]) + dot(up_rows, w_in_ref[1, :, cols])
        split_rows(value, cols, keep_ref, away_ref)


def merge_rows(part, fold_ref, keep_ref, other_ref, send_hbm, send_ref, sems):
    sources, _, width = send_ref.shape
    pieces = []
    for c in range(CHUNKS):
        cols = pl.ds(c * width, width)
        pieces.append((keep_ref[:, cols] + other_ref[:, cols].astype(F32)).astype(BF16))
    flat = jnp.concatenate(pieces, axis=0)
    each = sources // STEPS
    copies = []
    for step in range(STEPS):
        here = pl.ds(step * each, each)
        rows = dot(fold_ref[step * each * TILE : (step + 1) * each * TILE, :], flat).astype(BF16)
        send_ref[here] = rows.reshape(each, TILE, width)
        copies.append(
            pltpu.make_async_copy(
                send_ref.at[here], send_hbm.at[here, part * TILE : (part + 1) * TILE, :], sems.at[step]
            )
        )
        copies[-1].start()
    for copy in copies:
        copy.wait()


def merge_first_kernel(fold_ref, keep_ref, other_ref, send_hbm, send_ref, sems):
    merge_rows(0, fold_ref, keep_ref, other_ref, send_hbm, send_ref, sems)


def merge_second_kernel(fold_ref, keep_ref, other_ref, first_hbm, send_hbm, send_ref, sems):
    del first_hbm
    merge_rows(1, fold_ref, keep_ref, other_ref, send_hbm, send_ref, sems)


def weight_kernel(x_ref, c_ref, hid_ref, gg_ref, ug_ref, win_ref, wdown_ref):
    x = x_ref[...]
    win_ref[0] = dot(gg_ref[...], x).astype(BF16)
    win_ref[1] = dot(ug_ref[...], x).astype(BF16)
    wdown_ref[...] = dot(hid_ref[...], c_ref[...]).astype(BF16)


def combine_kernel(places, back_ref, pick_ref, weigh_ref, moe_hbm, grad_hbm, moe_ref, grad_ref, sems):
    width = back_ref.shape[2]
    rows = moe_ref.shape[0]
    reach = CHUNKS // STEPS
    copies = []
    for part, (table, out, home) in enumerate(
        ((weigh_ref, moe_ref, moe_hbm), (pick_ref, grad_ref, grad_hbm))
    ):
        lines = slice(part * TILE, (part + 1) * TILE)
        sums = []
        for spots in places:
            total = back_ref[spots[0], lines, :].astype(F32)
            for spot in spots[1:]:
                total = total + back_ref[spot, lines, :].astype(F32)
            sums.append(total.astype(BF16))
        flat = jnp.concatenate(sums, axis=0)
        for step in range(STEPS):
            low = step * reach
            wide = dot(table[low * rows : (low + reach) * rows, :], flat).astype(BF16)
            for c in range(reach):
                out[:, (low + c) * width : (low + c + 1) * width] = wide[c * rows : (c + 1) * rows]
            cols = pl.ds(low * width, reach * width)
            copies.append(pltpu.make_async_copy(out.at[:, cols], home.at[:, cols], sems.at[len(copies)]))
            copies[-1].start()
    for copy in copies:
        copy.wait()


def body(tokens, cotangent, expert_ids, gate_weights, w_in, w_down):
    groups, experts = lax.axis_size("row"), lax.axis_size("exp")
    rows, depth = tokens.shape
    width = depth // CHUNKS
    sources = groups * experts
    half = sources * CAP
    hidden = w_down.shape[1]
    w_in, w_down = in_hbm(w_in[0]), in_hbm(w_down[0])
    ids, gates = expert_ids.T, gate_weights.T
    order = [int(r) for r in np.random.RandomState(ORDER_SEED).permutation(sources)]
    owners = tuple(r % experts for r in order)
    places = tuple(
        tuple(order.index(g * experts + e) for g in range(groups)) for e in range(experts)
    )
    planes = [[(r // experts * PAIR + p) * experts + r % experts for r in order] for p in range(PAIR)]

    def exchange(array):
        return lax.all_to_all(
            array, ("row", "pair", "exp"), split_axis=0, concat_axis=0, tiled=True,
            axis_index_groups=planes,
        )

    def swap(array):
        return lax.ppermute(array, "pair", [(i, PAIR - 1 - i) for i in range(PAIR)])

    send = pl.pallas_call(
        functools.partial(gather_kernel, owners),
        out_shape=pltpu.VMEM((sources, 2 * TILE, width), BF16),
        in_specs=[hbm()] * 4,
        out_specs=vmem(),
        scratch_shapes=[
            pltpu.VMEM(ids.shape, ids.dtype),
            pltpu.VMEM(gates.shape, gates.dtype),
            pltpu.VMEM(tokens.shape, tokens.dtype),
            pltpu.VMEM(cotangent.shape, cotangent.dtype),
            pltpu.SemaphoreType.DMA((4,)),
        ],
        compiler_params=params(),
        name="gather_rows",
    )(in_hbm(ids), in_hbm(gates), in_hbm(tokens), in_hbm(cotangent))
    near = exchange(send)
    far = swap(near)
    square = pltpu.VMEM((sources * TILE, sources * TILE), BF16)
    w_in, x_near, c_near, unfolding, folding = pl.pallas_call(
        near_kernel,
        out_shape=(pltpu.VMEM(w_in.shape, BF16),)
        + (pltpu.VMEM((half, depth), BF16),) * 2
        + (square,) * 2,
        in_specs=[vmem(), hbm()],
        out_specs=[vmem()] * 5,
        scratch_shapes=[pltpu.SemaphoreType.DMA],
        compiler_params=params(),
        cost_estimate=cost(0, 4 * w_in.size),
        name="near_rows",
    )(near, w_in)
    wide = jax.ShapeDtypeStruct((2 * half, depth), BF16)
    tall = jax.ShapeDtypeStruct((hidden, 2 * half), BF16)
    slope = pltpu.VMEM(tall.shape, F32)
    x, hid, gate_slope, up_slope, w_down = pl.pallas_call(
        forward_kernel,
        out_shape=(wide, tall, slope, slope, pltpu.VMEM(w_down.shape, BF16)),
        in_specs=[vmem()] * 4 + [hbm()],
        out_specs=[vmem()] * 5,
        scratch_shapes=[pltpu.SemaphoreType.DMA],
        compiler_params=params(),
        name="gate_up",
    )(far, x_near, unfolding, w_in, w_down)
    halves = (pltpu.VMEM((half, depth), F32), pltpu.VMEM((half, depth), BF16))
    passes = 4 * hidden * depth * half
    keep_out, away_out = pl.pallas_call(
        down_kernel,
        out_shape=halves,
        in_specs=[vmem()] * 2,
        out_specs=[vmem()] * 2,
        compiler_params=params(),
        name="down",
    )(hid, w_down)
    other_out = swap(away_out)
    c, gg, ug = pl.pallas_call(
        hidden_kernel,
        out_shape=(wide, tall, tall),
        in_specs=[vmem()] * 6,
        out_specs=[vmem()] * 3,
        compiler_params=params(),
        cost_estimate=cost(passes, 2 * w_down.size),
        name="hidden_grad",
    )(far, c_near, unfolding, w_down, gate_slope, up_slope)
    keep_grad, away_grad = pl.pallas_call(
        back_kernel,
        out_shape=halves,
        in_specs=[vmem()] * 3,
        out_specs=[vmem()] * 2,
        compiler_params=params(),
        cost_estimate=cost(2 * passes, 2 * w_in.size),
        name="input_grad",
    )(gg, ug, w_in)
    other_grad = swap(away_grad)
    packet = pltpu.HBM((sources, 2 * TILE, width), BF16)
    staging = [pltpu.VMEM((sources, TILE, width), BF16), pltpu.SemaphoreType.DMA((STEPS,))]
    merged = pl.pallas_call(
        merge_first_kernel,
        out_shape=packet,
        in_specs=[vmem()] * 3,
        out_specs=hbm(),
        scratch_shapes=staging,
        compiler_params=params(),
        cost_estimate=cost(0, 8 * half * depth),
        name="merge_out",
    )(folding, keep_out, other_out)
    merged = pl.pallas_call(
        merge_second_kernel,
        out_shape=packet,
        in_specs=[vmem()] * 3 + [hbm()],
        out_specs=hbm(),
        scratch_shapes=staging,
        input_output_aliases={3: 0},
        compiler_params=params(),
        name="merge_grad",
    )(folding, keep_grad, other_grad, merged)
    back = exchange(merged)
    grad_in, grad_down = pl.pallas_call(
        weight_kernel,
        grid=(CHUNKS,),
        out_shape=(
            jax.ShapeDtypeStruct((2, hidden, depth), BF16),
            jax.ShapeDtypeStruct((hidden, depth), BF16),
        ),
        in_specs=[pl.BlockSpec((2 * half, width), lambda i: (0, i))] * 2
        + [pl.BlockSpec((hidden, 2 * half), lambda i: (0, 0))] * 3,
        out_specs=(
            pl.BlockSpec((2, hidden, width), lambda i: (0, 0, i)),
            pl.BlockSpec((hidden, width), lambda i: (0, i)),
        ),
        compiler_params=params(),
        cost_estimate=cost(3 * passes, 6 * hidden * depth + 8 * half * depth),
        name="weight_grads",
    )(x, c, hid, gg, ug)
    table = pltpu.VMEM((CHUNKS * rows, experts * TILE), BF16)
    pick, weigh = pl.pallas_call(
        table_kernel,
        out_shape=(table, table),
        in_specs=[vmem(), vmem(), pl.BlockSpec(memory_space=pl.ANY)],
        out_specs=[vmem()] * 2,
        compiler_params=params(),
        name="slot_tables",
    )(ids, gates, gg)
    moe_out, token_grad = pl.pallas_call(
        functools.partial(combine_kernel, places),
        out_shape=(pltpu.HBM((rows, depth), BF16),) * 2,
        in_specs=[vmem()] * 3,
        out_specs=[hbm()] * 2,
        scratch_shapes=[pltpu.VMEM((rows, depth), BF16)] * 2
        + [pltpu.SemaphoreType.DMA((2 * STEPS,))],
        compiler_params=params(),
        name="combine_rows",
    )(back, pick, weigh)
    return (moe_out, token_grad, grad_in[None], grad_down[None])


def solution(mesh):
    tok, exp = mesh.shape["tok"], mesh.shape["exp"]
    fine = Mesh(mesh.devices.reshape(tok // PAIR, PAIR, exp), ("row", "pair", "exp"))
    rows = P(("row", "pair", "exp"), None)
    win, wdown = P("exp", None, ("row", "pair"), None), P("exp", ("row", "pair"), None)
    return jax.shard_map(
        body,
        mesh=fine,
        in_specs=(rows, rows, rows, rows, win, wdown),
        out_specs=(rows, rows, win, wdown),
        check_vma=False,
    )
```

```python
import functools

import jax
import jax.numpy as jnp
import numpy as np
from jax import lax
from jax.experimental import pallas as pl
from jax.experimental.pallas import tpu as pltpu
from jax.sharding import Mesh, PartitionSpec as P

CAP = 2
TILE = 16
CHUNKS = TILE // CAP
PAIR = 2
STEPS = 2
ORDER_SEED = 2
F32 = jnp.float32
BF16 = jnp.bfloat16
LIMIT = 24 * 1024 * 1024


def iota(shape, dim):
    return lax.broadcasted_iota(jnp.int32, shape, dim)


def dot(a, b, dims=((1,), (0,))):
    return lax.dot_general(a, b, (dims, ((), ())), preferred_element_type=F32)


def vmem():
    return pl.BlockSpec(memory_space=pltpu.VMEM)


def hbm():
    return pl.BlockSpec(memory_space=pltpu.HBM)


def in_hbm(array):
    return pltpu.with_memory_space_constraint(array, pltpu.HBM)


def params():
    return pltpu.CompilerParams(vmem_limit_bytes=LIMIT)


def cost(flops, moved):
    return pl.CostEstimate(flops=flops, bytes_accessed=moved, transcendentals=0)


def slot_tables(ids, gates, experts):
    top, rows = ids.shape
    gates = gates.astype(F32)
    owner = iota((experts, rows), 0)
    member = jnp.zeros((experts, rows), F32)
    gate = jnp.zeros((experts, rows), F32)
    for k in range(top):
        hit = ids[k : k + 1, :] == owner
        member = member + jnp.where(hit, 1.0, 0.0)
        gate = gate + jnp.where(hit, gates[k : k + 1, :], 0.0)
    earlier = jnp.where(iota((rows, rows), 0) < iota((rows, rows), 1), 1.0, 0.0)
    slot = dot(member.astype(BF16), earlier.astype(BF16))
    picks = jnp.concatenate([jnp.where(slot == c, member, 0.0) for c in range(CAP)], axis=0)
    weights = jnp.concatenate([jnp.where(slot == c, gate, 0.0) for c in range(CAP)], axis=0)
    return picks.astype(BF16), weights.astype(BF16)


def message_masks(experts, rows):
    total = experts * TILE
    line = iota((total, CAP * experts), 0)
    spread = iota((total, CAP * experts), 1) == (line % CAP) * experts + line // TILE
    repeat = iota((rows, CHUNKS * rows), 1) % rows == iota((rows, CHUNKS * rows), 0)
    shape = (total, CHUNKS * rows)
    chunk = (iota(shape, 0) // CAP) % CHUNKS == iota(shape, 1) // rows
    return jnp.where(spread, 1.0, 0.0).astype(BF16), jnp.where(repeat, 1.0, 0.0).astype(BF16), chunk


def widen(table, masks):
    spread, repeat, chunk = masks
    small = dot(spread, table).astype(BF16)
    return jnp.where(chunk, dot(small, repeat), 0.0).astype(BF16)


def folded(ref, low, width):
    return jnp.concatenate(
        [ref[:, low + c * width : low + (c + 1) * width] for c in range(CHUNKS)], axis=0
    )


def gather_kernel(
    order, experts, ids_hbm, gates_hbm, tok_hbm, cot_hbm,
    send_ref,
    ids_ref, gates_ref, tok_ref, cot_ref, sems,
):
    rows, depth = tok_ref.shape
    width = depth // CHUNKS
    groups = len(order) // experts
    narrow = width // groups
    pairs = ((ids_hbm, ids_ref), (gates_hbm, gates_ref), (tok_hbm, tok_ref), (cot_hbm, cot_ref))
    copies = [pltpu.make_async_copy(a, b, sems.at[i]) for i, (a, b) in enumerate(pairs)]
    for copy in copies:
        copy.start()
    masks = message_masks(experts, rows)
    copies[0].wait()
    copies[1].wait()
    tables = slot_tables(ids_ref[...], gates_ref[...], experts)
    picks, weights = [widen(table, masks) for table in tables]
    shape = (experts, TILE, -1)
    copies[2].wait()
    moved = dot(picks, folded(tok_ref, 0, width)).astype(BF16).reshape(shape)
    for place, r in enumerate(order):
        send_ref[place, :, 0:width] = moved[r % experts]
    copies[3].wait()
    for g in range(groups):
        moved = dot(weights, folded(cot_ref, g * depth // groups, narrow)).astype(BF16).reshape(shape)
        for place, r in enumerate(order):
            if r // experts == g:
                send_ref[place, :, width : width + narrow] = moved[r % experts]


def table_kernel(ids_ref, gates_ref, after_ref, pick_ref, weigh_ref):
    del after_ref
    rows = ids_ref.shape[1]
    experts = pick_ref.shape[1] // TILE
    masks = message_masks(experts, rows)
    picks, weights = slot_tables(ids_ref[...], gates_ref[...], experts)
    pick_ref[...] = widen(picks, masks).T
    weigh_ref[...] = widen(weights, masks).T


def unfold(messages, perm, out):
    sources, _, width = messages.shape
    half = sources * CAP
    flat = dot(perm, messages.reshape(sources * TILE, width)).astype(BF16)
    for c in range(CHUNKS):
        out[:, c * width : (c + 1) * width] = flat[c * half : (c + 1) * half]


def near_kernel(near_ref, w_in_hbm, w_in_ref, x_ref, c_ref, unfold_ref, fold_ref, sem):
    fetch = pltpu.make_async_copy(w_in_hbm, w_in_ref, sem)
    fetch.start()
    sources = near_ref.shape[0]
    width = x_ref.shape[1] // CHUNKS
    half, lines = sources * CAP, sources * TILE
    row, col = iota((lines, lines), 0), iota((lines, lines), 1)
    perm = (row % half // CAP) * TILE + (row // half) * CAP + row % CAP == col
    perm = jnp.where(perm, 1.0, 0.0).astype(BF16)
    unfold_ref[...] = perm
    back = (row // CAP % CHUNKS) * half + (row // TILE) * CAP + row % CAP == col
    fold_ref[...] = jnp.where(back, 1.0, 0.0).astype(BF16)
    unfold(near_ref[:, :, 0:width], perm, x_ref)
    unfold(near_ref[:, :, width:], perm, c_ref)
    fetch.wait()


def forward_kernel(
    far_ref, x_near, unfold_ref, w_in_ref, w_down_hbm,
    x_ref, hid_ref, gate_slope_ref, up_slope_ref, w_down_ref, sem,
):
    fetch = pltpu.make_async_copy(w_down_hbm, w_down_ref, sem)
    fetch.start()
    hidden = w_down_ref.shape[0]
    half = far_ref.shape[0] * CAP
    x_ref[0:half, :] = x_near[...]
    width = x_ref.shape[1] // CHUNKS
    unfold(far_ref[:, :, 0:width], unfold_ref[...], x_ref.at[half : 2 * half])
    both = dot(w_in_ref[...].reshape(2 * hidden, -1), x_ref[...], ((1,), (1,)))
    gate, up = both[:hidden], both[hidden:]
    sig = jax.nn.sigmoid(gate)
    silu = gate * sig
    hid_ref[...] = (silu * up).astype(BF16)
    gate_slope_ref[...] = up * sig * (1.0 + gate * (1.0 - sig))
    up_slope_ref[...] = silu
    fetch.wait()


def split_rows(value, cols, keep_ref, away_ref):
    half = keep_ref.shape[0]
    keep_ref[:, cols] = value[:half]
    away_ref[:, cols] = value[half:].astype(BF16)


def down_kernel(hid_ref, w_down_ref, keep_ref, away_ref):
    width = w_down_ref.shape[1] // CHUNKS
    rows = hid_ref[...].T
    for c in range(CHUNKS):
        cols = pl.ds(c * width, width)
        split_rows(dot(rows, w_down_ref[:, cols]), cols, keep_ref, away_ref)


def hidden_kernel(groups, *refs):
    others, refs = refs[: 2 * (groups - 1)], refs[2 * (groups - 1) :]
    far_ref, c_near, unfold_ref, w_down_ref, gate_slope_ref, up_slope_ref, c_ref, gg_ref, ug_ref = refs
    half, share = c_near.shape
    width = c_ref.shape[1] // CHUNKS
    narrow = share // CHUNKS
    near_rows, far_rows = c_ref.at[0:half], c_ref.at[half : 2 * half]
    plane = lax.axis_index("row")
    bases = [pl.multiple_of(lax.rem(plane + k, groups) * share, share) for k in range(groups)]
    near_rows[:, pl.ds(bases[0], share)] = c_near[...]
    homes = [(far_rows, bases[0])]
    for base in bases[1:]:
        homes += [(near_rows, base), (far_rows, base)]
    lines = unfold_ref.shape[0]
    messages = [far_ref[:, :, width:]] + [other[...] for other in others]
    flat = jnp.concatenate([m.reshape(lines, narrow) for m in messages], axis=1)
    flat = dot(unfold_ref[...], flat).astype(BF16)
    for i, (rows, base) in enumerate(homes):
        for c in range(CHUNKS):
            rows[:, pl.ds(base + c * narrow, narrow)] = flat[
                c * half : (c + 1) * half, i * narrow : (i + 1) * narrow
            ]
    grad = dot(w_down_ref[...], c_ref[...], ((1,), (1,)))
    gg_ref[...] = (grad * gate_slope_ref[...]).astype(BF16)
    ug_ref[...] = (grad * up_slope_ref[...]).astype(BF16)


def back_kernel(gg_ref, ug_ref, w_in_ref, keep_ref, away_ref):
    width = w_in_ref.shape[2] // CHUNKS
    gate_rows, up_rows = gg_ref[...].T, ug_ref[...].T
    for c in range(CHUNKS):
        cols = pl.ds(c * width, width)
        value = dot(gate_rows, w_in_ref[0, :, cols]) + dot(up_rows, w_in_ref[1, :, cols])
        split_rows(value, cols, keep_ref, away_ref)


def merge_rows(part, fold_ref, keep_ref, other_ref, send_hbm, send_ref, sems):
    sources, _, width = send_ref.shape
    pieces = []
    for c in range(CHUNKS):
        cols = pl.ds(c * width, width)
        pieces.append((keep_ref[:, cols] + other_ref[:, cols].astype(F32)).astype(BF16))
    flat = jnp.concatenate(pieces, axis=0)
    each = sources // STEPS
    copies = []
    for step in range(STEPS):
        here = pl.ds(step * each, each)
        rows = dot(fold_ref[step * each * TILE : (step + 1) * each * TILE, :], flat).astype(BF16)
        send_ref[here] = rows.reshape(each, TILE, width)
        copies.append(
            pltpu.make_async_copy(
                send_ref.at[here], send_hbm.at[here, part * TILE : (part + 1) * TILE, :], sems.at[step]
            )
        )
        copies[-1].start()
    for copy in copies:
        copy.wait()


def merge_first_kernel(fold_ref, keep_ref, other_ref, send_hbm, send_ref, sems):
    merge_rows(0, fold_ref, keep_ref, other_ref, send_hbm, send_ref, sems)


def merge_second_kernel(fold_ref, keep_ref, other_ref, first_hbm, send_hbm, send_ref, sems):
    del first_hbm
    merge_rows(1, fold_ref, keep_ref, other_ref, send_hbm, send_ref, sems)


def weight_kernel(x_ref, c_ref, hid_ref, gg_ref, ug_ref, win_ref, wdown_ref):
    x = x_ref[...]
    win_ref[0] = dot(gg_ref[...], x).astype(BF16)
    win_ref[1] = dot(ug_ref[...], x).astype(BF16)
    wdown_ref[...] = dot(hid_ref[...], c_ref[...]).astype(BF16)


def combine_kernel(places, back_ref, pick_ref, weigh_ref, moe_hbm, grad_hbm, moe_ref, grad_ref, sems):
    width = back_ref.shape[2]
    rows = moe_ref.shape[0]
    reach = CHUNKS // STEPS
    copies = []
    for part, (table, out, home) in enumerate(
        ((weigh_ref, moe_ref, moe_hbm), (pick_ref, grad_ref, grad_hbm))
    ):
        lines = slice(part * TILE, (part + 1) * TILE)
        sums = []
        for spots in places:
            total = back_ref[spots[0], lines, :].astype(F32)
            for spot in spots[1:]:
                total = total + back_ref[spot, lines, :].astype(F32)
            sums.append(total.astype(BF16))
        flat = jnp.concatenate(sums, axis=0)
        for step in range(STEPS):
            low = step * reach
            wide = dot(table[low * rows : (low + reach) * rows, :], flat).astype(BF16)
            for c in range(reach):
                out[:, (low + c) * width : (low + c + 1) * width] = wide[c * rows : (c + 1) * rows]
            cols = pl.ds(low * width, reach * width)
            copies.append(pltpu.make_async_copy(out.at[:, cols], home.at[:, cols], sems.at[len(copies)]))
            copies[-1].start()
    for copy in copies:
        copy.wait()


def body(tokens, cotangent, expert_ids, gate_weights, w_in, w_down):
    groups, experts = lax.axis_size("row"), lax.axis_size("exp")
    rows, depth = tokens.shape
    width = depth // CHUNKS
    sources = groups * experts
    half = sources * CAP
    hidden = w_down.shape[1]
    w_in, w_down = in_hbm(w_in[0]), in_hbm(w_down[0])
    ids, gates = expert_ids.T, gate_weights.T
    order = [int(r) for r in np.random.RandomState(ORDER_SEED).permutation(sources)]
    places = tuple(
        tuple(order.index(g * experts + e) for g in range(groups)) for e in range(experts)
    )
    planes = [[(r // experts * PAIR + p) * experts + r % experts for r in order] for p in range(PAIR)]

    def exchange(array):
        return lax.all_to_all(
            array, ("row", "pair", "exp"), split_axis=0, concat_axis=0, tiled=True,
            axis_index_groups=planes,
        )

    def swap(array):
        return lax.ppermute(array, "pair", [(i, PAIR - 1 - i) for i in range(PAIR)])

    send = pl.pallas_call(
        functools.partial(gather_kernel, order, experts),
        out_shape=pltpu.VMEM((sources, TILE, width + width // groups), BF16),
        in_specs=[hbm()] * 4,
        out_specs=vmem(),
        scratch_shapes=[
            pltpu.VMEM(ids.shape, ids.dtype),
            pltpu.VMEM(gates.shape, gates.dtype),
            pltpu.VMEM(tokens.shape, tokens.dtype),
            pltpu.VMEM(cotangent.shape, cotangent.dtype),
            pltpu.SemaphoreType.DMA((4,)),
        ],
        compiler_params=params(),
        name="gather_rows",
    )(in_hbm(ids), in_hbm(gates), in_hbm(tokens), in_hbm(cotangent))
    near = exchange(send)
    far = swap(near)
    share = near[:, :, width:]
    turned = [
        lax.ppermute(share, "row", [((i + k) % groups, i) for i in range(groups)])
        for k in range(1, groups)
    ]
    square = pltpu.VMEM((sources * TILE, sources * TILE), BF16)
    w_in, x_near, c_near, unfolding, folding = pl.pallas_call(
        near_kernel,
        out_shape=(pltpu.VMEM(w_in.shape, BF16),)
        + (pltpu.VMEM((half, depth), BF16), pltpu.VMEM((half, depth // groups), BF16))
        + (square,) * 2,
        in_specs=[vmem(), hbm()],
        out_specs=[vmem()] * 5,
        scratch_shapes=[pltpu.SemaphoreType.DMA],
        compiler_params=params(),
        cost_estimate=cost(0, 4 * w_in.size),
        name="near_rows",
    )(near, w_in)
    wide = jax.ShapeDtypeStruct((2 * half, depth), BF16)
    tall = jax.ShapeDtypeStruct((hidden, 2 * half), BF16)
    slope = pltpu.VMEM(tall.shape, F32)
    x, hid, gate_slope, up_slope, w_down = pl.pallas_call(
        forward_kernel,
        out_shape=(wide, tall, slope, slope, pltpu.VMEM(w_down.shape, BF16)),
        in_specs=[vmem()] * 4 + [hbm()],
        out_specs=[vmem()] * 5,
        scratch_shapes=[pltpu.SemaphoreType.DMA],
        compiler_params=params(),
        name="gate_up",
    )(far, x_near, unfolding, w_in, w_down)
    hid, turned = lax.optimization_barrier((hid, turned))
    others = [other for array in turned for other in (array, swap(array))]
    halves = (pltpu.VMEM((half, depth), F32), pltpu.VMEM((half, depth), BF16))
    passes = 4 * hidden * depth * half
    keep_out, away_out = pl.pallas_call(
        down_kernel,
        out_shape=halves,
        in_specs=[vmem()] * 2,
        out_specs=[vmem()] * 2,
        compiler_params=params(),
        name="down",
    )(hid, w_down)
    other_out = swap(away_out)
    c, gg, ug = pl.pallas_call(
        functools.partial(hidden_kernel, groups),
        out_shape=(wide, tall, tall),
        in_specs=[vmem()] * (6 + len(others)),
        out_specs=[vmem()] * 3,
        compiler_params=params(),
        cost_estimate=cost(passes, 2 * w_down.size),
        name="hidden_grad",
    )(*others, far, c_near, unfolding, w_down, gate_slope, up_slope)
    keep_grad, away_grad = pl.pallas_call(
        back_kernel,
        out_shape=halves,
        in_specs=[vmem()] * 3,
        out_specs=[vmem()] * 2,
        compiler_params=params(),
        cost_estimate=cost(2 * passes, 2 * w_in.size),
        name="input_grad",
    )(gg, ug, w_in)
    other_grad = swap(away_grad)
    packet = pltpu.HBM((sources, 2 * TILE, width), BF16)
    staging = [pltpu.VMEM((sources, TILE, width), BF16), pltpu.SemaphoreType.DMA((STEPS,))]
    merged = pl.pallas_call(
        merge_first_kernel,
        out_shape=packet,
        in_specs=[vmem()] * 3,
        out_specs=hbm(),
        scratch_shapes=staging,
        compiler_params=params(),
        cost_estimate=cost(0, 8 * half * depth),
        name="merge_out",
    )(folding, keep_out, other_out)
    merged = pl.pallas_call(
        merge_second_kernel,
        out_shape=packet,
        in_specs=[vmem()] * 3 + [hbm()],
        out_specs=hbm(),
        scratch_shapes=staging,
        input_output_aliases={3: 0},
        compiler_params=params(),
        name="merge_grad",
    )(folding, keep_grad, other_grad, merged)
    back = exchange(merged)
    grad_in, grad_down = pl.pallas_call(
        weight_kernel,
        grid=(CHUNKS,),
        out_shape=(
            jax.ShapeDtypeStruct((2, hidden, depth), BF16),
            jax.ShapeDtypeStruct((hidden, depth), BF16),
        ),
        in_specs=[pl.BlockSpec((2 * half, width), lambda i: (0, i))] * 2
        + [pl.BlockSpec((hidden, 2 * half), lambda i: (0, 0))] * 3,
        out_specs=(
            pl.BlockSpec((2, hidden, width), lambda i: (0, 0, i)),
            pl.BlockSpec((hidden, width), lambda i: (0, i)),
        ),
        compiler_params=params(),
        cost_estimate=cost(3 * passes, 6 * hidden * depth + 8 * half * depth),
        name="weight_grads",
    )(x, c, hid, gg, ug)
    table = pltpu.VMEM((CHUNKS * rows, experts * TILE), BF16)
    pick, weigh = pl.pallas_call(
        table_kernel,
        out_shape=(table, table),
        in_specs=[vmem(), vmem(), pl.BlockSpec(memory_space=pl.ANY)],
        out_specs=[vmem()] * 2,
        compiler_params=params(),
        name="slot_tables",
    )(ids, gates, gg)
    moe_out, token_grad = pl.pallas_call(
        functools.partial(combine_kernel, places),
        out_shape=(pltpu.HBM((rows, depth), BF16),) * 2,
        in_specs=[vmem()] * 3,
        out_specs=[hbm()] * 2,
        scratch_shapes=[pltpu.VMEM((rows, depth), BF16)] * 2
        + [pltpu.SemaphoreType.DMA((2 * STEPS,))],
        compiler_params=params(),
        name="combine_rows",
    )(back, pick, weigh)
    return (moe_out, token_grad, grad_in[None], grad_down[None])


def solution(mesh):
    tok, exp = mesh.shape["tok"], mesh.shape["exp"]
    fine = Mesh(mesh.devices.reshape(tok // PAIR, PAIR, exp), ("row", "pair", "exp"))
    rows = P(("row", "pair", "exp"), None)
    win, wdown = P("exp", None, ("row", "pair"), None), P("exp", ("row", "pair"), None)
    return jax.shard_map(
        body,
        mesh=fine,
        in_specs=(rows, rows, rows, rows, win, wdown),
        out_specs=(rows, rows, win, wdown),
        check_vma=False,
    )
```

```python
import functools

import jax
import jax.numpy as jnp
import numpy as np
from jax import lax
from jax.experimental import pallas as pl
from jax.experimental.pallas import tpu as pltpu
from jax.sharding import Mesh, PartitionSpec as P

CAP = 2
TILE = 16
CHUNKS = TILE // CAP
PAIR = 2
STEPS = 2
SEEDS = (40, 2)
F32 = jnp.float32
BF16 = jnp.bfloat16
LIMIT = 24 * 1024 * 1024


def iota(shape, dim):
    return lax.broadcasted_iota(jnp.int32, shape, dim)


def dot(a, b, dims=((1,), (0,))):
    return lax.dot_general(a, b, (dims, ((), ())), preferred_element_type=F32)


def vmem():
    return pl.BlockSpec(memory_space=pltpu.VMEM)


def hbm():
    return pl.BlockSpec(memory_space=pltpu.HBM)


def in_hbm(array):
    return pltpu.with_memory_space_constraint(array, pltpu.HBM)


def params():
    return pltpu.CompilerParams(vmem_limit_bytes=LIMIT)


def cost(flops, moved):
    return pl.CostEstimate(flops=flops, bytes_accessed=moved, transcendentals=0)


def slot_tables(ids, gates, experts):
    top, rows = ids.shape
    gates = gates.astype(F32)
    owner = iota((experts, rows), 0)
    member = jnp.zeros((experts, rows), F32)
    gate = jnp.zeros((experts, rows), F32)
    for k in range(top):
        hit = ids[k : k + 1, :] == owner
        member = member + jnp.where(hit, 1.0, 0.0)
        gate = gate + jnp.where(hit, gates[k : k + 1, :], 0.0)
    earlier = jnp.where(iota((rows, rows), 0) < iota((rows, rows), 1), 1.0, 0.0)
    slot = dot(member.astype(BF16), earlier.astype(BF16))
    picks = jnp.concatenate([jnp.where(slot == c, member, 0.0) for c in range(CAP)], axis=0)
    weights = jnp.concatenate([jnp.where(slot == c, gate, 0.0) for c in range(CAP)], axis=0)
    return picks.astype(BF16), weights.astype(BF16)


def message_masks(experts, rows):
    total = experts * TILE
    line = iota((total, CAP * experts), 0)
    spread = iota((total, CAP * experts), 1) == (line % CAP) * experts + line // TILE
    repeat = iota((rows, CHUNKS * rows), 1) % rows == iota((rows, CHUNKS * rows), 0)
    shape = (total, CHUNKS * rows)
    chunk = (iota(shape, 0) // CAP) % CHUNKS == iota(shape, 1) // rows
    return jnp.where(spread, 1.0, 0.0).astype(BF16), jnp.where(repeat, 1.0, 0.0).astype(BF16), chunk


def widen(table, masks):
    spread, repeat, chunk = masks
    small = dot(spread, table).astype(BF16)
    return jnp.where(chunk, dot(small, repeat), 0.0).astype(BF16)


def folded(ref, low, width):
    return jnp.concatenate(
        [ref[:, low + c * width : low + (c + 1) * width] for c in range(CHUNKS)], axis=0
    )


def gather_kernel(
    order, experts, ids_hbm, gates_hbm, tok_hbm, cot_hbm,
    send_ref,
    ids_ref, gates_ref, tok_ref, cot_ref, sems,
):
    rows, depth = tok_ref.shape
    width = depth // CHUNKS
    groups = len(order) // experts
    narrow = width // groups
    pairs = ((ids_hbm, ids_ref), (gates_hbm, gates_ref), (tok_hbm, tok_ref), (cot_hbm, cot_ref))
    copies = [pltpu.make_async_copy(a, b, sems.at[i]) for i, (a, b) in enumerate(pairs)]
    for copy in copies:
        copy.start()
    masks = message_masks(experts, rows)
    copies[0].wait()
    copies[1].wait()
    tables = slot_tables(ids_ref[...], gates_ref[...], experts)
    picks, weights = [widen(table, masks) for table in tables]
    shape = (experts, TILE, -1)
    copies[2].wait()
    moved = dot(picks, folded(tok_ref, 0, width)).astype(BF16).reshape(shape)
    for place, r in enumerate(order):
        send_ref[place, :, 0:width] = moved[r % experts]
    copies[3].wait()
    for g in range(groups):
        moved = dot(weights, folded(cot_ref, g * depth // groups, narrow)).astype(BF16).reshape(shape)
        for place, r in enumerate(order):
            if r // experts == g:
                send_ref[place, :, width : width + narrow] = moved[r % experts]


def table_kernel(ids_ref, gates_ref, after_ref, pick_ref, weigh_ref):
    del after_ref
    rows = ids_ref.shape[1]
    experts = pick_ref.shape[1] // TILE
    masks = message_masks(experts, rows)
    picks, weights = slot_tables(ids_ref[...], gates_ref[...], experts)
    pick_ref[...] = widen(picks, masks).T
    weigh_ref[...] = widen(weights, masks).T


def unfold(messages, perm, out):
    sources, _, width = messages.shape
    half = sources * CAP
    flat = dot(perm, messages.reshape(sources * TILE, width)).astype(BF16)
    for c in range(CHUNKS):
        out[:, c * width : (c + 1) * width] = flat[c * half : (c + 1) * half]


def near_kernel(
    origins, near_ref, far_ref, w_in_hbm, w_in_ref, x_ref, c_ref, unfold_ref, fold_ref, sem
):
    fetch = pltpu.make_async_copy(w_in_hbm, w_in_ref, sem)
    fetch.start()
    sources = near_ref.shape[0]
    width = x_ref.shape[1] // CHUNKS
    half, lines = sources * CAP, sources * TILE
    row, col = iota((lines, lines), 0), iota((lines, lines), 1)
    perm = (row % half // CAP) * TILE + (row // half) * CAP + row % CAP == col
    perm = jnp.where(perm, 1.0, 0.0).astype(BF16)
    unfold_ref[...] = perm
    for side, ref in enumerate((near_ref, far_ref)):
        rows = slice(side * half, (side + 1) * half)
        unfold(ref[:, :, 0:width], perm, x_ref.at[rows])
        unfold(ref[:, :, width:], perm, c_ref.at[rows])
    row, col = iota((TILE, lines), 0), iota((TILE, lines), 1)
    place = row // CAP * half + row % CAP
    for p, s in enumerate(origins):
        tile = jnp.where(place + s * CAP == col, 1.0, 0.0).astype(BF16)
        fold_ref[p * TILE : (p + 1) * TILE, :] = tile
    fetch.wait()


def forward_kernel(
    x_ref, w_in_ref, w_down_hbm, hid_ref, gate_slope_ref, up_slope_ref, w_down_ref, sem
):
    fetch = pltpu.make_async_copy(w_down_hbm, w_down_ref, sem)
    fetch.start()
    hidden = w_down_ref.shape[0]
    both = dot(w_in_ref[...].reshape(2 * hidden, -1), x_ref[...], ((1,), (1,)))
    gate, up = both[:hidden], both[hidden:]
    sig = jax.nn.sigmoid(gate)
    silu = gate * sig
    hid_ref[...] = (silu * up).astype(BF16)
    gate_slope_ref[...] = up * sig * (1.0 + gate * (1.0 - sig))
    up_slope_ref[...] = silu
    fetch.wait()


def split_rows(value, cols, keep_ref, away_ref):
    half = keep_ref.shape[0]
    keep_ref[:, cols] = value[:half]
    away_ref[:, cols] = value[half:].astype(BF16)


def down_kernel(hid_ref, w_down_ref, keep_ref, away_ref):
    width = w_down_ref.shape[1] // CHUNKS
    rows = hid_ref[...].T
    for c in range(CHUNKS):
        cols = pl.ds(c * width, width)
        split_rows(dot(rows, w_down_ref[:, cols]), cols, keep_ref, away_ref)


def hidden_kernel(groups, *refs):
    others, refs = refs[: 2 * (groups - 1)], refs[2 * (groups - 1) :]
    c_own, unfold_ref, w_down_ref, gate_slope_ref, up_slope_ref, c_ref, gg_ref, ug_ref = refs
    share = c_own.shape[1]
    half = c_own.shape[0] // 2
    narrow = share // CHUNKS
    plane = lax.axis_index("row")
    bases = [pl.multiple_of(lax.rem(plane + k, groups) * share, share) for k in range(groups)]
    c_ref[:, pl.ds(bases[0], share)] = c_own[...]
    if others:
        lines = unfold_ref.shape[0]
        flat = jnp.concatenate([other[...].reshape(lines, narrow) for other in others], axis=1)
        flat = dot(unfold_ref[...], flat).astype(BF16)
        for i in range(len(others)):
            rows = c_ref.at[i % 2 * half : (i % 2 + 1) * half]
            for c in range(CHUNKS):
                rows[:, pl.ds(bases[1 + i // 2] + c * narrow, narrow)] = flat[
                    c * half : (c + 1) * half, i * narrow : (i + 1) * narrow
                ]
    grad = dot(w_down_ref[...], c_ref[...], ((1,), (1,)))
    gg_ref[...] = (grad * gate_slope_ref[...]).astype(BF16)
    ug_ref[...] = (grad * up_slope_ref[...]).astype(BF16)


def back_kernel(gg_ref, ug_ref, w_in_ref, keep_ref, away_ref):
    width = w_in_ref.shape[2] // CHUNKS
    gate_rows, up_rows = gg_ref[...].T, ug_ref[...].T
    for c in range(CHUNKS):
        cols = pl.ds(c * width, width)
        value = dot(gate_rows, w_in_ref[0, :, cols]) + dot(up_rows, w_in_ref[1, :, cols])
        split_rows(value, cols, keep_ref, away_ref)


def merge_rows(part, fold_ref, keep_ref, other_ref, send_hbm, send_ref, sems):
    sources, _, width = send_ref.shape
    pieces = []
    for c in range(CHUNKS):
        cols = pl.ds(c * width, width)
        pieces.append((keep_ref[:, cols] + other_ref[:, cols].astype(F32)).astype(BF16))
    flat = jnp.concatenate(pieces, axis=0)
    each = sources // STEPS
    copies = []
    for step in range(STEPS):
        here = pl.ds(step * each, each)
        rows = dot(fold_ref[step * each * TILE : (step + 1) * each * TILE, :], flat).astype(BF16)
        send_ref[here] = rows.reshape(each, TILE, width)
        copies.append(
            pltpu.make_async_copy(
                send_ref.at[here], send_hbm.at[here, part * TILE : (part + 1) * TILE, :], sems.at[step]
            )
        )
        copies[-1].start()
    for copy in copies:
        copy.wait()


def merge_first_kernel(fold_ref, keep_ref, other_ref, send_hbm, send_ref, sems):
    merge_rows(0, fold_ref, keep_ref, other_ref, send_hbm, send_ref, sems)


def merge_second_kernel(fold_ref, keep_ref, other_ref, first_hbm, send_hbm, send_ref, sems):
    del first_hbm
    merge_rows(1, fold_ref, keep_ref, other_ref, send_hbm, send_ref, sems)


def weight_kernel(x_ref, c_ref, hid_ref, gg_ref, ug_ref, win_ref, wdown_ref):
    x = x_ref[...]
    win_ref[0] = dot(gg_ref[...], x).astype(BF16)
    win_ref[1] = dot(ug_ref[...], x).astype(BF16)
    wdown_ref[...] = dot(hid_ref[...], c_ref[...]).astype(BF16)


def combine_kernel(places, back_ref, pick_ref, weigh_ref, moe_hbm, grad_hbm, moe_ref, grad_ref, sems):
    width = back_ref.shape[2]
    rows = moe_ref.shape[0]
    reach = CHUNKS // STEPS
    copies = []
    for part, (table, out, home) in enumerate(
        ((weigh_ref, moe_ref, moe_hbm), (pick_ref, grad_ref, grad_hbm))
    ):
        lines = slice(part * TILE, (part + 1) * TILE)
        sums = []
        for spots in places:
            total = back_ref[spots[0], lines, :].astype(F32)
            for spot in spots[1:]:
                total = total + back_ref[spot, lines, :].astype(F32)
            sums.append(total.astype(BF16))
        flat = jnp.concatenate(sums, axis=0)
        for step in range(STEPS):
            low = step * reach
            wide = dot(table[low * rows : (low + reach) * rows, :], flat).astype(BF16)
            for c in range(reach):
                out[:, (low + c) * width : (low + c + 1) * width] = wide[c * rows : (c + 1) * rows]
            cols = pl.ds(low * width, reach * width)
            copies.append(pltpu.make_async_copy(out.at[:, cols], home.at[:, cols], sems.at[len(copies)]))
            copies[-1].start()
    for copy in copies:
        copy.wait()


def body(tokens, cotangent, expert_ids, gate_weights, w_in, w_down):
    groups, experts = lax.axis_size("row"), lax.axis_size("exp")
    rows, depth = tokens.shape
    width = depth // CHUNKS
    sources = groups * experts
    half = sources * CAP
    hidden = w_down.shape[1]
    w_in, w_down = in_hbm(w_in[0]), in_hbm(w_down[0])
    ids, gates = expert_ids.T, gate_weights.T
    orders = [[int(r) for r in np.random.RandomState(seed).permutation(sources)] for seed in SEEDS]
    places = tuple(
        tuple(orders[1].index(g * experts + e) for g in range(groups)) for e in range(experts)
    )

    def exchange(array, order):
        planes = [
            [(r // experts * PAIR + p) * experts + r % experts for r in order] for p in range(PAIR)
        ]
        return lax.all_to_all(
            array, ("row", "pair", "exp"), split_axis=0, concat_axis=0, tiled=True,
            axis_index_groups=planes,
        )

    def swap(array):
        return lax.ppermute(array, "pair", [(i, PAIR - 1 - i) for i in range(PAIR)])

    send = pl.pallas_call(
        functools.partial(gather_kernel, orders[0], experts),
        out_shape=pltpu.VMEM((sources, TILE, width + width // groups), BF16),
        in_specs=[hbm()] * 4,
        out_specs=vmem(),
        scratch_shapes=[
            pltpu.VMEM(ids.shape, ids.dtype),
            pltpu.VMEM(gates.shape, gates.dtype),
            pltpu.VMEM(tokens.shape, tokens.dtype),
            pltpu.VMEM(cotangent.shape, cotangent.dtype),
            pltpu.SemaphoreType.DMA((4,)),
        ],
        compiler_params=params(),
        name="gather_rows",
    )(in_hbm(ids), in_hbm(gates), in_hbm(tokens), in_hbm(cotangent))
    near = exchange(send, orders[0])
    far = swap(near)
    share = near[:, :, width:]
    turned = [
        lax.ppermute(share, "row", [((i + k) % groups, i) for i in range(groups)])
        for k in range(1, groups)
    ]
    square = pltpu.VMEM((sources * TILE, sources * TILE), BF16)
    wide = jax.ShapeDtypeStruct((2 * half, depth), BF16)
    tall = jax.ShapeDtypeStruct((hidden, 2 * half), BF16)
    w_in, x, c_own, unfolding, folding = pl.pallas_call(
        functools.partial(near_kernel, tuple(orders[0].index(r) for r in orders[1])),
        out_shape=(
            pltpu.VMEM(w_in.shape, BF16), wide, pltpu.VMEM((2 * half, depth // groups), BF16),
            square, square,
        ),
        in_specs=[vmem()] * 2 + [hbm()],
        out_specs=[vmem()] * 5,
        scratch_shapes=[pltpu.SemaphoreType.DMA],
        compiler_params=params(),
        cost_estimate=cost(0, 4 * w_in.size),
        name="near_rows",
    )(near, far, w_in)
    slope = pltpu.VMEM(tall.shape, F32)
    hid, gate_slope, up_slope, w_down = pl.pallas_call(
        forward_kernel,
        out_shape=(tall, slope, slope, pltpu.VMEM(w_down.shape, BF16)),
        in_specs=[vmem()] * 2 + [hbm()],
        out_specs=[vmem()] * 4,
        scratch_shapes=[pltpu.SemaphoreType.DMA],
        compiler_params=params(),
        name="gate_up",
    )(x, w_in, w_down)
    hid, turned = lax.optimization_barrier((hid, turned))
    others = [other for array in turned for other in (array, swap(array))]
    halves = (pltpu.VMEM((half, depth), F32), pltpu.VMEM((half, depth), BF16))
    passes = 4 * hidden * depth * half
    keep_out, away_out = pl.pallas_call(
        down_kernel,
        out_shape=halves,
        in_specs=[vmem()] * 2,
        out_specs=[vmem()] * 2,
        compiler_params=params(),
        name="down",
    )(hid, w_down)
    other_out = swap(away_out)
    c, gg, ug = pl.pallas_call(
        functools.partial(hidden_kernel, groups),
        out_shape=(wide, tall, tall),
        in_specs=[vmem()] * (5 + len(others)),
        out_specs=[vmem()] * 3,
        compiler_params=params(),
        cost_estimate=cost(passes, 2 * w_down.size),
        name="hidden_grad",
    )(*others, c_own, unfolding, w_down, gate_slope, up_slope)
    keep_grad, away_grad = pl.pallas_call(
        back_kernel,
        out_shape=halves,
        in_specs=[vmem()] * 3,
        out_specs=[vmem()] * 2,
        compiler_params=params(),
        cost_estimate=cost(2 * passes, 2 * w_in.size),
        name="input_grad",
    )(gg, ug, w_in)
    other_grad = swap(away_grad)
    packet = pltpu.HBM((sources, 2 * TILE, width), BF16)
    staging = [pltpu.VMEM((sources, TILE, width), BF16), pltpu.SemaphoreType.DMA((STEPS,))]
    merged = pl.pallas_call(
        merge_first_kernel,
        out_shape=packet,
        in_specs=[vmem()] * 3,
        out_specs=hbm(),
        scratch_shapes=staging,
        compiler_params=params(),
        cost_estimate=cost(0, 8 * half * depth),
        name="merge_out",
    )(folding, keep_out, other_out)
    merged = pl.pallas_call(
        merge_second_kernel,
        out_shape=packet,
        in_specs=[vmem()] * 3 + [hbm()],
        out_specs=hbm(),
        scratch_shapes=staging,
        input_output_aliases={3: 0},
        compiler_params=params(),
        name="merge_grad",
    )(folding, keep_grad, other_grad, merged)
    back = exchange(merged, orders[1])
    grad_in, grad_down = pl.pallas_call(
        weight_kernel,
        grid=(CHUNKS,),
        out_shape=(
            jax.ShapeDtypeStruct((2, hidden, depth), BF16),
            jax.ShapeDtypeStruct((hidden, depth), BF16),
        ),
        in_specs=[pl.BlockSpec((2 * half, width), lambda i: (0, i))] * 2
        + [pl.BlockSpec((hidden, 2 * half), lambda i: (0, 0))] * 3,
        out_specs=(
            pl.BlockSpec((2, hidden, width), lambda i: (0, 0, i)),
            pl.BlockSpec((hidden, width), lambda i: (0, i)),
        ),
        compiler_params=params(),
        cost_estimate=cost(3 * passes, 6 * hidden * depth + 8 * half * depth),
        name="weight_grads",
    )(x, c, hid, gg, ug)
    table = pltpu.VMEM((CHUNKS * rows, experts * TILE), BF16)
    pick, weigh = pl.pallas_call(
        table_kernel,
        out_shape=(table, table),
        in_specs=[vmem(), vmem(), pl.BlockSpec(memory_space=pl.ANY)],
        out_specs=[vmem()] * 2,
        compiler_params=params(),
        name="slot_tables",
    )(ids, gates, gg)
    moe_out, token_grad = pl.pallas_call(
        functools.partial(combine_kernel, places),
        out_shape=(pltpu.HBM((rows, depth), BF16),) * 2,
        in_specs=[vmem()] * 3,
        out_specs=[hbm()] * 2,
        scratch_shapes=[pltpu.VMEM((rows, depth), BF16)] * 2
        + [pltpu.SemaphoreType.DMA((2 * STEPS,))],
        compiler_params=params(),
        name="combine_rows",
    )(back, pick, weigh)
    return (moe_out, token_grad, grad_in[None], grad_down[None])


def solution(mesh):
    tok, exp = mesh.shape["tok"], mesh.shape["exp"]
    fine = Mesh(mesh.devices.reshape(tok // PAIR, PAIR, exp), ("row", "pair", "exp"))
    rows = P(("row", "pair", "exp"), None)
    win, wdown = P("exp", None, ("row", "pair"), None), P("exp", ("row", "pair"), None)
    return jax.shard_map(
        body,
        mesh=fine,
        in_specs=(rows, rows, rows, rows, win, wdown),
        out_specs=(rows, rows, win, wdown),
        check_vma=False,
    )
```

```python
import functools

import jax
import jax.numpy as jnp
import numpy as np
from jax import lax
from jax.experimental import pallas as pl
from jax.experimental.pallas import tpu as pltpu
from jax.sharding import Mesh, PartitionSpec as P

CAP = 2
TILE = 16
CHUNKS = TILE // CAP
PAIR = 2
STEPS = 2
SEEDS = (40, 2)
F32 = jnp.float32
BF16 = jnp.bfloat16
LIMIT = 24 * 1024 * 1024


def iota(shape, dim):
    return lax.broadcasted_iota(jnp.int32, shape, dim)


def dot(a, b, dims=((1,), (0,))):
    return lax.dot_general(a, b, (dims, ((), ())), preferred_element_type=F32)


def vmem():
    return pl.BlockSpec(memory_space=pltpu.VMEM)


def hbm():
    return pl.BlockSpec(memory_space=pltpu.HBM)


def in_hbm(array):
    return pltpu.with_memory_space_constraint(array, pltpu.HBM)


def params():
    return pltpu.CompilerParams(vmem_limit_bytes=LIMIT)


def cost(flops, moved):
    return pl.CostEstimate(flops=flops, bytes_accessed=moved, transcendentals=0)


def slot_tables(ids, gates, experts):
    top, rows = ids.shape
    gates = gates.astype(F32)
    owner = iota((experts, rows), 0)
    member = jnp.zeros((experts, rows), F32)
    gate = jnp.zeros((experts, rows), F32)
    for k in range(top):
        hit = ids[k : k + 1, :] == owner
        member = member + jnp.where(hit, 1.0, 0.0)
        gate = gate + jnp.where(hit, gates[k : k + 1, :], 0.0)
    earlier = jnp.where(iota((rows, rows), 0) < iota((rows, rows), 1), 1.0, 0.0)
    slot = dot(member.astype(BF16), earlier.astype(BF16))
    picks = jnp.concatenate([jnp.where(slot == c, member, 0.0) for c in range(CAP)], axis=0)
    weights = jnp.concatenate([jnp.where(slot == c, gate, 0.0) for c in range(CAP)], axis=0)
    return picks.astype(BF16), weights.astype(BF16)


def message_masks(experts, rows):
    total = experts * TILE
    line = iota((total, CAP * experts), 0)
    spread = iota((total, CAP * experts), 1) == (line % CAP) * experts + line // TILE
    repeat = iota((rows, CHUNKS * rows), 1) % rows == iota((rows, CHUNKS * rows), 0)
    shape = (total, CHUNKS * rows)
    chunk = (iota(shape, 0) // CAP) % CHUNKS == iota(shape, 1) // rows
    return jnp.where(spread, 1.0, 0.0).astype(BF16), jnp.where(repeat, 1.0, 0.0).astype(BF16), chunk


def widen(table, masks):
    spread, repeat, chunk = masks
    small = dot(spread, table).astype(BF16)
    return jnp.where(chunk, dot(small, repeat), 0.0).astype(BF16)


def folded(ref, low, width):
    return jnp.concatenate(
        [ref[:, low + c * width : low + (c + 1) * width] for c in range(CHUNKS)], axis=0
    )


def gather_kernel(
    order, experts, ids_hbm, gates_hbm, tok_hbm, cot_hbm,
    send_ref,
    ids_ref, gates_ref, tok_ref, cot_ref, sems,
):
    rows, depth = tok_ref.shape
    width = depth // CHUNKS
    groups = len(order) // experts
    narrow = width // groups
    pairs = ((ids_hbm, ids_ref), (gates_hbm, gates_ref), (tok_hbm, tok_ref), (cot_hbm, cot_ref))
    copies = [pltpu.make_async_copy(a, b, sems.at[i]) for i, (a, b) in enumerate(pairs)]
    for copy in copies:
        copy.start()
    masks = message_masks(experts, rows)
    copies[0].wait()
    copies[1].wait()
    tables = slot_tables(ids_ref[...], gates_ref[...], experts)
    picks, weights = [widen(table, masks) for table in tables]
    shape = (experts, TILE, -1)
    copies[2].wait()
    moved = dot(picks, folded(tok_ref, 0, width)).astype(BF16).reshape(shape)
    for place, r in enumerate(order):
        send_ref[place, :, 0:width] = moved[r % experts]
    copies[3].wait()
    for g in range(groups):
        moved = dot(weights, folded(cot_ref, g * depth // groups, narrow)).astype(BF16).reshape(shape)
        for place, r in enumerate(order):
            if r // experts == g:
                send_ref[place, :, width : width + narrow] = moved[r % experts]


def table_kernel(ids_ref, gates_ref, after_ref, pick_ref, weigh_ref):
    del after_ref
    rows = ids_ref.shape[1]
    experts = pick_ref.shape[1] // TILE
    masks = message_masks(experts, rows)
    picks, weights = slot_tables(ids_ref[...], gates_ref[...], experts)
    pick_ref[...] = widen(picks, masks).T
    weigh_ref[...] = widen(weights, masks).T


def unfold(messages, perm, out):
    sources, _, width = messages.shape
    half = sources * CAP
    flat = dot(perm, messages.reshape(sources * TILE, width)).astype(BF16)
    for c in range(CHUNKS):
        out[:, c * width : (c + 1) * width] = flat[c * half : (c + 1) * half]


def near_kernel(origins, near_ref, w_in_hbm, w_in_ref, x_ref, c_ref, unfold_ref, fold_ref, sem):
    fetch = pltpu.make_async_copy(w_in_hbm, w_in_ref, sem)
    fetch.start()
    sources = near_ref.shape[0]
    width = x_ref.shape[1] // CHUNKS
    half, lines = sources * CAP, sources * TILE
    row, col = iota((lines, lines), 0), iota((lines, lines), 1)
    perm = (row % half // CAP) * TILE + (row // half) * CAP + row % CAP == col
    perm = jnp.where(perm, 1.0, 0.0).astype(BF16)
    unfold_ref[...] = perm
    unfold(near_ref[:, :, 0:width], perm, x_ref)
    unfold(near_ref[:, :, width:], perm, c_ref)
    row, col = iota((TILE, lines), 0), iota((TILE, lines), 1)
    place = row // CAP * half + row % CAP
    for p, s in enumerate(origins):
        tile = jnp.where(place + s * CAP == col, 1.0, 0.0).astype(BF16)
        fold_ref[p * TILE : (p + 1) * TILE, :] = tile
    fetch.wait()


def forward_kernel(
    far_ref, x_near, unfold_ref, w_in_ref, w_down_hbm,
    x_ref, hid_ref, gate_slope_ref, up_slope_ref, w_down_ref, sem,
):
    fetch = pltpu.make_async_copy(w_down_hbm, w_down_ref, sem)
    fetch.start()
    hidden = w_down_ref.shape[0]
    half = far_ref.shape[0] * CAP
    x_ref[0:half, :] = x_near[...]
    width = x_ref.shape[1] // CHUNKS
    unfold(far_ref[:, :, 0:width], unfold_ref[...], x_ref.at[half : 2 * half])
    both = dot(w_in_ref[...].reshape(2 * hidden, -1), x_ref[...], ((1,), (1,)))
    gate, up = both[:hidden], both[hidden:]
    sig = jax.nn.sigmoid(gate)
    silu = gate * sig
    hid_ref[...] = (silu * up).astype(BF16)
    gate_slope_ref[...] = up * sig * (1.0 + gate * (1.0 - sig))
    up_slope_ref[...] = silu
    fetch.wait()


def split_rows(value, cols, keep_ref, away_ref):
    half = keep_ref.shape[0]
    keep_ref[:, cols] = value[:half]
    away_ref[:, cols] = value[half:].astype(BF16)


def down_kernel(hid_ref, w_down_ref, keep_ref, away_ref):
    width = w_down_ref.shape[1] // CHUNKS
    rows = hid_ref[...].T
    for c in range(CHUNKS):
        cols = pl.ds(c * width, width)
        split_rows(dot(rows, w_down_ref[:, cols]), cols, keep_ref, away_ref)


def hidden_kernel(groups, *refs):
    others, refs = refs[: 2 * (groups - 1)], refs[2 * (groups - 1) :]
    far_ref, c_near, unfold_ref, w_down_ref, gate_slope_ref, up_slope_ref, c_ref, gg_ref, ug_ref = refs
    half, share = c_near.shape
    width = c_ref.shape[1] // CHUNKS
    narrow = share // CHUNKS
    near_rows, far_rows = c_ref.at[0:half], c_ref.at[half : 2 * half]
    plane = lax.axis_index("row")
    bases = [pl.multiple_of(lax.rem(plane + k, groups) * share, share) for k in range(groups)]
    near_rows[:, pl.ds(bases[0], share)] = c_near[...]
    homes = [(far_rows, bases[0])]
    for base in bases[1:]:
        homes += [(near_rows, base), (far_rows, base)]
    lines = unfold_ref.shape[0]
    messages = [far_ref[:, :, width:]] + [other[...] for other in others]
    flat = jnp.concatenate([m.reshape(lines, narrow) for m in messages], axis=1)
    flat = dot(unfold_ref[...], flat).astype(BF16)
    for i, (rows, base) in enumerate(homes):
        for c in range(CHUNKS):
            rows[:, pl.ds(base + c * narrow, narrow)] = flat[
                c * half : (c + 1) * half, i * narrow : (i + 1) * narrow
            ]
    grad = dot(w_down_ref[...], c_ref[...], ((1,), (1,)))
    gg_ref[...] = (grad * gate_slope_ref[...]).astype(BF16)
    ug_ref[...] = (grad * up_slope_ref[...]).astype(BF16)


def back_kernel(gg_ref, ug_ref, w_in_ref, keep_ref, away_ref):
    width = w_in_ref.shape[2] // CHUNKS
    gate_rows, up_rows = gg_ref[...].T, ug_ref[...].T
    for c in range(CHUNKS):
        cols = pl.ds(c * width, width)
        value = dot(gate_rows, w_in_ref[0, :, cols]) + dot(up_rows, w_in_ref[1, :, cols])
        split_rows(value, cols, keep_ref, away_ref)


def merge_rows(part, fold_ref, keep_ref, other_ref, send_hbm, send_ref, sems):
    sources, _, width = send_ref.shape
    pieces = []
    for c in range(CHUNKS):
        cols = pl.ds(c * width, width)
        pieces.append((keep_ref[:, cols] + other_ref[:, cols].astype(F32)).astype(BF16))
    flat = jnp.concatenate(pieces, axis=0)
    each = sources // STEPS
    copies = []
    for step in range(STEPS):
        here = pl.ds(step * each, each)
        rows = dot(fold_ref[step * each * TILE : (step + 1) * each * TILE, :], flat).astype(BF16)
        send_ref[here] = rows.reshape(each, TILE, width)
        copies.append(
            pltpu.make_async_copy(
                send_ref.at[here], send_hbm.at[here, part * TILE : (part + 1) * TILE, :], sems.at[step]
            )
        )
        copies[-1].start()
    for copy in copies:
        copy.wait()


def merge_first_kernel(fold_ref, keep_ref, other_ref, send_hbm, send_ref, sems):
    merge_rows(0, fold_ref, keep_ref, other_ref, send_hbm, send_ref, sems)


def merge_second_kernel(fold_ref, keep_ref, other_ref, first_hbm, send_hbm, send_ref, sems):
    del first_hbm
    merge_rows(1, fold_ref, keep_ref, other_ref, send_hbm, send_ref, sems)


def weight_kernel(x_ref, c_ref, hid_ref, gg_ref, ug_ref, win_ref, wdown_ref):
    x = x_ref[...]
    win_ref[0] = dot(gg_ref[...], x).astype(BF16)
    win_ref[1] = dot(ug_ref[...], x).astype(BF16)
    wdown_ref[...] = dot(hid_ref[...], c_ref[...]).astype(BF16)


def combine_kernel(places, back_ref, pick_ref, weigh_ref, moe_hbm, grad_hbm, moe_ref, grad_ref, sems):
    width = back_ref.shape[2]
    rows = moe_ref.shape[0]
    reach = CHUNKS // STEPS
    copies = []
    for part, (table, out, home) in enumerate(
        ((weigh_ref, moe_ref, moe_hbm), (pick_ref, grad_ref, grad_hbm))
    ):
        lines = slice(part * TILE, (part + 1) * TILE)
        sums = []
        for spots in places:
            total = back_ref[spots[0], lines, :].astype(F32)
            for spot in spots[1:]:
                total = total + back_ref[spot, lines, :].astype(F32)
            sums.append(total.astype(BF16))
        flat = jnp.concatenate(sums, axis=0)
        for step in range(STEPS):
            low = step * reach
            wide = dot(table[low * rows : (low + reach) * rows, :], flat).astype(BF16)
            for c in range(reach):
                out[:, (low + c) * width : (low + c + 1) * width] = wide[c * rows : (c + 1) * rows]
            cols = pl.ds(low * width, reach * width)
            copies.append(pltpu.make_async_copy(out.at[:, cols], home.at[:, cols], sems.at[len(copies)]))
            copies[-1].start()
    for copy in copies:
        copy.wait()


def body(tokens, cotangent, expert_ids, gate_weights, w_in, w_down):
    groups, experts = lax.axis_size("row"), lax.axis_size("exp")
    rows, depth = tokens.shape
    width = depth // CHUNKS
    sources = groups * experts
    half = sources * CAP
    hidden = w_down.shape[1]
    w_in, w_down = in_hbm(w_in[0]), in_hbm(w_down[0])
    ids, gates = expert_ids.T, gate_weights.T
    orders = [[int(r) for r in np.random.RandomState(seed).permutation(sources)] for seed in SEEDS]
    places = tuple(
        tuple(orders[1].index(g * experts + e) for g in range(groups)) for e in range(experts)
    )

    def exchange(array, order):
        planes = [
            [(r // experts * PAIR + p) * experts + r % experts for r in order] for p in range(PAIR)
        ]
        return lax.all_to_all(
            array, ("row", "pair", "exp"), split_axis=0, concat_axis=0, tiled=True,
            axis_index_groups=planes,
        )

    def swap(array):
        return lax.ppermute(array, "pair", [(i, PAIR - 1 - i) for i in range(PAIR)])

    send = pl.pallas_call(
        functools.partial(gather_kernel, orders[0], experts),
        out_shape=pltpu.VMEM((sources, TILE, width + width // groups), BF16),
        in_specs=[hbm()] * 4,
        out_specs=vmem(),
        scratch_shapes=[
            pltpu.VMEM(ids.shape, ids.dtype),
            pltpu.VMEM(gates.shape, gates.dtype),
            pltpu.VMEM(tokens.shape, tokens.dtype),
            pltpu.VMEM(cotangent.shape, cotangent.dtype),
            pltpu.SemaphoreType.DMA((4,)),
        ],
        compiler_params=params(),
        name="gather_rows",
    )(in_hbm(ids), in_hbm(gates), in_hbm(tokens), in_hbm(cotangent))
    near = exchange(send, orders[0])
    far = swap(near)
    share = near[:, :, width:]
    turned = [
        lax.ppermute(share, "row", [((i + k) % groups, i) for i in range(groups)])
        for k in range(1, groups)
    ]
    square = pltpu.VMEM((sources * TILE, sources * TILE), BF16)
    wide = jax.ShapeDtypeStruct((2 * half, depth), BF16)
    tall = jax.ShapeDtypeStruct((hidden, 2 * half), BF16)
    w_in, x_near, c_near, unfolding, folding = pl.pallas_call(
        functools.partial(near_kernel, tuple(orders[0].index(r) for r in orders[1])),
        out_shape=(
            pltpu.VMEM(w_in.shape, BF16), pltpu.VMEM((half, depth), BF16),
            pltpu.VMEM((half, depth // groups), BF16), square, square,
        ),
        in_specs=[vmem(), hbm()],
        out_specs=[vmem()] * 5,
        scratch_shapes=[pltpu.SemaphoreType.DMA],
        compiler_params=params(),
        cost_estimate=cost(0, 4 * w_in.size),
        name="near_rows",
    )(near, w_in)
    slope = pltpu.VMEM(tall.shape, F32)
    x, hid, gate_slope, up_slope, w_down = pl.pallas_call(
        forward_kernel,
        out_shape=(wide, tall, slope, slope, pltpu.VMEM(w_down.shape, BF16)),
        in_specs=[vmem()] * 4 + [hbm()],
        out_specs=[vmem()] * 5,
        scratch_shapes=[pltpu.SemaphoreType.DMA],
        compiler_params=params(),
        name="gate_up",
    )(far, x_near, unfolding, w_in, w_down)
    hid, turned = lax.optimization_barrier((hid, turned))
    others = [other for array in turned for other in (array, swap(array))]
    halves = (pltpu.VMEM((half, depth), F32), pltpu.VMEM((half, depth), BF16))
    passes = 4 * hidden * depth * half
    keep_out, away_out = pl.pallas_call(
        down_kernel,
        out_shape=halves,
        in_specs=[vmem()] * 2,
        out_specs=[vmem()] * 2,
        compiler_params=params(),
        name="down",
    )(hid, w_down)
    other_out = swap(away_out)
    c, gg, ug = pl.pallas_call(
        functools.partial(hidden_kernel, groups),
        out_shape=(wide, tall, tall),
        in_specs=[vmem()] * (6 + len(others)),
        out_specs=[vmem()] * 3,
        compiler_params=params(),
        cost_estimate=cost(passes, 2 * w_down.size),
        name="hidden_grad",
    )(*others, far, c_near, unfolding, w_down, gate_slope, up_slope)
    keep_grad, away_grad = pl.pallas_call(
        back_kernel,
        out_shape=halves,
        in_specs=[vmem()] * 3,
        out_specs=[vmem()] * 2,
        compiler_params=params(),
        cost_estimate=cost(2 * passes, 2 * w_in.size),
        name="input_grad",
    )(gg, ug, w_in)
    other_grad = swap(away_grad)
    packet = pltpu.HBM((sources, 2 * TILE, width), BF16)
    staging = [pltpu.VMEM((sources, TILE, width), BF16), pltpu.SemaphoreType.DMA((STEPS,))]
    merged = pl.pallas_call(
        merge_first_kernel,
        out_shape=packet,
        in_specs=[vmem()] * 3,
        out_specs=hbm(),
        scratch_shapes=staging,
        compiler_params=params(),
        cost_estimate=cost(0, 8 * half * depth),
        name="merge_out",
    )(folding, keep_out, other_out)
    merged = pl.pallas_call(
        merge_second_kernel,
        out_shape=packet,
        in_specs=[vmem()] * 3 + [hbm()],
        out_specs=hbm(),
        scratch_shapes=staging,
        input_output_aliases={3: 0},
        compiler_params=params(),
        name="merge_grad",
    )(folding, keep_grad, other_grad, merged)
    back = exchange(merged, orders[1])
    grad_in, grad_down = pl.pallas_call(
        weight_kernel,
        grid=(CHUNKS,),
        out_shape=(
            jax.ShapeDtypeStruct((2, hidden, depth), BF16),
            jax.ShapeDtypeStruct((hidden, depth), BF16),
        ),
        in_specs=[pl.BlockSpec((2 * half, width), lambda i: (0, i))] * 2
        + [pl.BlockSpec((hidden, 2 * half), lambda i: (0, 0))] * 3,
        out_specs=(
            pl.BlockSpec((2, hidden, width), lambda i: (0, 0, i)),
            pl.BlockSpec((hidden, width), lambda i: (0, i)),
        ),
        compiler_params=params(),
        cost_estimate=cost(3 * passes, 6 * hidden * depth + 8 * half * depth),
        name="weight_grads",
    )(x, c, hid, gg, ug)
    table = pltpu.VMEM((CHUNKS * rows, experts * TILE), BF16)
    pick, weigh = pl.pallas_call(
        table_kernel,
        out_shape=(table, table),
        in_specs=[vmem(), vmem(), pl.BlockSpec(memory_space=pl.ANY)],
        out_specs=[vmem()] * 2,
        compiler_params=params(),
        name="slot_tables",
    )(ids, gates, gg)
    moe_out, token_grad = pl.pallas_call(
        functools.partial(combine_kernel, places),
        out_shape=(pltpu.HBM((rows, depth), BF16),) * 2,
        in_specs=[vmem()] * 3,
        out_specs=[hbm()] * 2,
        scratch_shapes=[pltpu.VMEM((rows, depth), BF16)] * 2
        + [pltpu.SemaphoreType.DMA((2 * STEPS,))],
        compiler_params=params(),
        name="combine_rows",
    )(back, pick, weigh)
    return (moe_out, token_grad, grad_in[None], grad_down[None])


def solution(mesh):
    tok, exp = mesh.shape["tok"], mesh.shape["exp"]
    fine = Mesh(mesh.devices.reshape(tok // PAIR, PAIR, exp), ("row", "pair", "exp"))
    rows = P(("row", "pair", "exp"), None)
    win, wdown = P("exp", None, ("row", "pair"), None), P("exp", ("row", "pair"), None)
    return jax.shard_map(
        body,
        mesh=fine,
        in_specs=(rows, rows, rows, rows, win, wdown),
        out_specs=(rows, rows, win, wdown),
        check_vma=False,
    )
```

```python
import functools

import jax
import jax.numpy as jnp
import numpy as np
from jax import lax
from jax.experimental import pallas as pl
from jax.experimental.pallas import tpu as pltpu
from jax.sharding import Mesh, PartitionSpec as P

CAP = 2
TILE = 16
CHUNKS = TILE // CAP
PAIR = 2
STEPS = 2
SEEDS = (40, 4)
F32 = jnp.float32
BF16 = jnp.bfloat16
LIMIT = 24 * 1024 * 1024


def iota(shape, dim):
    return lax.broadcasted_iota(jnp.int32, shape, dim)


def dot(a, b, dims=((1,), (0,))):
    return lax.dot_general(a, b, (dims, ((), ())), preferred_element_type=F32)


def vmem():
    return pl.BlockSpec(memory_space=pltpu.VMEM)


def hbm():
    return pl.BlockSpec(memory_space=pltpu.HBM)


def in_hbm(array):
    return pltpu.with_memory_space_constraint(array, pltpu.HBM)


def params():
    return pltpu.CompilerParams(vmem_limit_bytes=LIMIT)


def cost(flops, moved):
    return pl.CostEstimate(flops=flops, bytes_accessed=moved, transcendentals=0)


def slot_tables(ids, gates, experts):
    top, rows = ids.shape
    gates = gates.astype(F32)
    owner = iota((experts, rows), 0)
    member = jnp.zeros((experts, rows), F32)
    gate = jnp.zeros((experts, rows), F32)
    for k in range(top):
        hit = ids[k : k + 1, :] == owner
        member = member + jnp.where(hit, 1.0, 0.0)
        gate = gate + jnp.where(hit, gates[k : k + 1, :], 0.0)
    earlier = jnp.where(iota((rows, rows), 0) < iota((rows, rows), 1), 1.0, 0.0)
    slot = dot(member.astype(BF16), earlier.astype(BF16))
    picks = jnp.concatenate([jnp.where(slot == c, member, 0.0) for c in range(CAP)], axis=0)
    weights = jnp.concatenate([jnp.where(slot == c, gate, 0.0) for c in range(CAP)], axis=0)
    return picks.astype(BF16), weights.astype(BF16)


def message_masks(experts, rows):
    total = experts * TILE
    line = iota((total, CAP * experts), 0)
    spread = iota((total, CAP * experts), 1) == (line % CAP) * experts + line // TILE
    repeat = iota((rows, CHUNKS * rows), 1) % rows == iota((rows, CHUNKS * rows), 0)
    shape = (total, CHUNKS * rows)
    chunk = (iota(shape, 0) // CAP) % CHUNKS == iota(shape, 1) // rows
    return jnp.where(spread, 1.0, 0.0).astype(BF16), jnp.where(repeat, 1.0, 0.0).astype(BF16), chunk


def widen(table, masks):
    spread, repeat, chunk = masks
    small = dot(spread, table).astype(BF16)
    return jnp.where(chunk, dot(small, repeat), 0.0).astype(BF16)


def folded(ref, low, width):
    return jnp.concatenate(
        [ref[:, low + c * width : low + (c + 1) * width] for c in range(CHUNKS)], axis=0
    )


def gather_kernel(
    order, experts, ids_hbm, gates_hbm, tok_hbm, cot_hbm,
    send_ref,
    ids_ref, gates_ref, tok_ref, cot_ref, sems,
):
    rows, depth = tok_ref.shape
    width = depth // CHUNKS
    groups = len(order) // experts
    narrow = width // groups
    pairs = ((ids_hbm, ids_ref), (gates_hbm, gates_ref), (tok_hbm, tok_ref), (cot_hbm, cot_ref))
    copies = [pltpu.make_async_copy(a, b, sems.at[i]) for i, (a, b) in enumerate(pairs)]
    for copy in copies:
        copy.start()
    masks = message_masks(experts, rows)
    copies[0].wait()
    copies[1].wait()
    tables = slot_tables(ids_ref[...], gates_ref[...], experts)
    picks, weights = [widen(table, masks) for table in tables]
    shape = (experts, TILE, -1)
    copies[2].wait()
    moved = dot(picks, folded(tok_ref, 0, width)).astype(BF16).reshape(shape)
    for place, r in enumerate(order):
        send_ref[place, :, 0:width] = moved[r % experts]
    copies[3].wait()
    for g in range(groups):
        moved = dot(weights, folded(cot_ref, g * depth // groups, narrow)).astype(BF16).reshape(shape)
        for place, r in enumerate(order):
            if r // experts == g:
                send_ref[place, :, width : width + narrow] = moved[r % experts]


def table_kernel(ids_ref, gates_ref, after_ref, pick_ref, weigh_ref):
    del after_ref
    rows = ids_ref.shape[1]
    experts = pick_ref.shape[1] // TILE
    masks = message_masks(experts, rows)
    picks, weights = slot_tables(ids_ref[...], gates_ref[...], experts)
    pick_ref[...] = widen(picks, masks).T
    weigh_ref[...] = widen(weights, masks).T


def unfold(messages, perm, out):
    sources, _, width = messages.shape
    half = sources * CAP
    flat = dot(perm, messages.reshape(sources * TILE, width)).astype(BF16)
    for c in range(CHUNKS):
        out[:, c * width : (c + 1) * width] = flat[c * half : (c + 1) * half]


def near_kernel(origins, near_ref, w_in_hbm, w_in_ref, x_ref, c_ref, unfold_ref, fold_ref, sem):
    fetch = pltpu.make_async_copy(w_in_hbm, w_in_ref, sem)
    fetch.start()
    sources = near_ref.shape[0]
    width = x_ref.shape[1] // CHUNKS
    half, lines = sources * CAP, sources * TILE
    row, col = iota((lines, lines), 0), iota((lines, lines), 1)
    perm = (row % half // CAP) * TILE + (row // half) * CAP + row % CAP == col
    perm = jnp.where(perm, 1.0, 0.0).astype(BF16)
    unfold_ref[...] = perm
    unfold(near_ref[:, :, 0:width], perm, x_ref)
    unfold(near_ref[:, :, width:], perm, c_ref)
    row, col = iota((TILE, lines), 0), iota((TILE, lines), 1)
    place = row // CAP * half + row % CAP
    for p, s in enumerate(origins):
        tile = jnp.where(place + s * CAP == col, 1.0, 0.0).astype(BF16)
        fold_ref[p * TILE : (p + 1) * TILE, :] = tile
    fetch.wait()


def forward_kernel(
    far_ref, x_near, unfold_ref, w_in_ref, w_down_hbm,
    x_ref, hid_ref, gate_slope_ref, up_slope_ref, w_down_ref, sem,
):
    fetch = pltpu.make_async_copy(w_down_hbm, w_down_ref, sem)
    fetch.start()
    hidden = w_down_ref.shape[0]
    half = far_ref.shape[0] * CAP
    x_ref[0:half, :] = x_near[...]
    width = x_ref.shape[1] // CHUNKS
    unfold(far_ref[:, :, 0:width], unfold_ref[...], x_ref.at[half : 2 * half])
    both = dot(w_in_ref[...].reshape(2 * hidden, -1), x_ref[...], ((1,), (1,)))
    gate, up = both[:hidden], both[hidden:]
    sig = jax.nn.sigmoid(gate)
    silu = gate * sig
    hid_ref[...] = (silu * up).astype(BF16)
    gate_slope_ref[...] = up * sig * (1.0 + gate * (1.0 - sig))
    up_slope_ref[...] = silu
    fetch.wait()


def split_rows(value, cols, keep_ref, away_ref):
    half = keep_ref.shape[0]
    keep_ref[:, cols] = value[:half]
    away_ref[:, cols] = value[half:].astype(BF16)


def down_kernel(hid_ref, w_down_ref, keep_ref, away_ref):
    width = w_down_ref.shape[1] // CHUNKS
    rows = hid_ref[...].T
    for c in range(CHUNKS):
        cols = pl.ds(c * width, width)
        split_rows(dot(rows, w_down_ref[:, cols]), cols, keep_ref, away_ref)


def hidden_kernel(groups, *refs):
    others, refs = refs[: 2 * (groups - 1)], refs[2 * (groups - 1) :]
    far_ref, c_near, unfold_ref, w_down_ref, gate_slope_ref, up_slope_ref, c_ref, gg_ref, ug_ref = refs
    half, share = c_near.shape
    width = c_ref.shape[1] // CHUNKS
    narrow = share // CHUNKS
    near_rows, far_rows = c_ref.at[0:half], c_ref.at[half : 2 * half]
    plane = lax.axis_index("row")
    bases = [pl.multiple_of(lax.rem(plane + k, groups) * share, share) for k in range(groups)]
    near_rows[:, pl.ds(bases[0], share)] = c_near[...]
    homes = [(far_rows, bases[0])]
    for base in bases[1:]:
        homes += [(near_rows, base), (far_rows, base)]
    lines = unfold_ref.shape[0]
    messages = [far_ref[:, :, width:]] + [other[...] for other in others]
    flat = jnp.concatenate([m.reshape(lines, narrow) for m in messages], axis=1)
    flat = dot(unfold_ref[...], flat).astype(BF16)
    for i, (rows, base) in enumerate(homes):
        for c in range(CHUNKS):
            rows[:, pl.ds(base + c * narrow, narrow)] = flat[
                c * half : (c + 1) * half, i * narrow : (i + 1) * narrow
            ]
    grad = dot(w_down_ref[...], c_ref[...], ((1,), (1,)))
    gg_ref[...] = (grad * gate_slope_ref[...]).astype(BF16)
    ug_ref[...] = (grad * up_slope_ref[...]).astype(BF16)


def back_kernel(gg_ref, ug_ref, w_in_ref, keep_ref, away_ref):
    width = w_in_ref.shape[2] // CHUNKS
    gate_rows, up_rows = gg_ref[...].T, ug_ref[...].T
    for c in range(CHUNKS):
        cols = pl.ds(c * width, width)
        value = dot(gate_rows, w_in_ref[0, :, cols]) + dot(up_rows, w_in_ref[1, :, cols])
        split_rows(value, cols, keep_ref, away_ref)


def merge_rows(part, fold_ref, keep_ref, other_ref, send_hbm, send_ref, sems):
    sources, _, width = send_ref.shape
    pieces = []
    for c in range(CHUNKS):
        cols = pl.ds(c * width, width)
        pieces.append((keep_ref[:, cols] + other_ref[:, cols].astype(F32)).astype(BF16))
    flat = jnp.concatenate(pieces, axis=0)
    each = sources // STEPS
    copies = []
    for step in range(STEPS):
        here = pl.ds(step * each, each)
        rows = dot(fold_ref[step * each * TILE : (step + 1) * each * TILE, :], flat).astype(BF16)
        send_ref[here] = rows.reshape(each, TILE, width)
        copies.append(
            pltpu.make_async_copy(
                send_ref.at[here], send_hbm.at[here, part * TILE : (part + 1) * TILE, :], sems.at[step]
            )
        )
        copies[-1].start()
    for copy in copies:
        copy.wait()


def merge_first_kernel(fold_ref, keep_ref, other_ref, send_hbm, send_ref, sems):
    merge_rows(0, fold_ref, keep_ref, other_ref, send_hbm, send_ref, sems)


def merge_second_kernel(fold_ref, keep_ref, other_ref, first_hbm, send_hbm, send_ref, sems):
    del first_hbm
    merge_rows(1, fold_ref, keep_ref, other_ref, send_hbm, send_ref, sems)


def weight_kernel(x_ref, c_ref, hid_ref, gg_ref, ug_ref, win_ref, wdown_ref):
    x = x_ref[...]
    win_ref[0] = dot(gg_ref[...], x).astype(BF16)
    win_ref[1] = dot(ug_ref[...], x).astype(BF16)
    wdown_ref[...] = dot(hid_ref[...], c_ref[...]).astype(BF16)


def combine_kernel(places, back_ref, pick_ref, weigh_ref, moe_hbm, grad_hbm, moe_ref, grad_ref, sems):
    width = back_ref.shape[2]
    rows = moe_ref.shape[0]
    reach = CHUNKS // STEPS
    copies = []
    for part, (table, out, home) in enumerate(
        ((weigh_ref, moe_ref, moe_hbm), (pick_ref, grad_ref, grad_hbm))
    ):
        lines = slice(part * TILE, (part + 1) * TILE)
        sums = []
        for spots in places:
            total = back_ref[spots[0], lines, :].astype(F32)
            for spot in spots[1:]:
                total = total + back_ref[spot, lines, :].astype(F32)
            sums.append(total.astype(BF16))
        flat = jnp.concatenate(sums, axis=0)
        for step in range(STEPS):
            low = step * reach
            wide = dot(table[low * rows : (low + reach) * rows, :], flat).astype(BF16)
            for c in range(reach):
                out[:, (low + c) * width : (low + c + 1) * width] = wide[c * rows : (c + 1) * rows]
            cols = pl.ds(low * width, reach * width)
            copies.append(pltpu.make_async_copy(out.at[:, cols], home.at[:, cols], sems.at[len(copies)]))
            copies[-1].start()
    for copy in copies:
        copy.wait()


def body(tokens, cotangent, expert_ids, gate_weights, w_in, w_down):
    groups, experts = lax.axis_size("row"), lax.axis_size("exp")
    rows, depth = tokens.shape
    width = depth // CHUNKS
    sources = groups * experts
    half = sources * CAP
    hidden = w_down.shape[1]
    w_in, w_down = in_hbm(w_in[0]), in_hbm(w_down[0])
    ids, gates = expert_ids.T, gate_weights.T
    orders = [[int(r) for r in np.random.RandomState(seed).permutation(sources)] for seed in SEEDS]
    places = tuple(
        tuple(orders[1].index(g * experts + e) for g in range(groups)) for e in range(experts)
    )

    def exchange(array, order):
        planes = [
            [(r // experts * PAIR + p) * experts + r % experts for r in order] for p in range(PAIR)
        ]
        return lax.all_to_all(
            array, ("row", "pair", "exp"), split_axis=0, concat_axis=0, tiled=True,
            axis_index_groups=planes,
        )

    def swap(array):
        return lax.ppermute(array, "pair", [(i, PAIR - 1 - i) for i in range(PAIR)])

    send = pl.pallas_call(
        functools.partial(gather_kernel, orders[0], experts),
        out_shape=pltpu.VMEM((sources, TILE, width + width // groups), BF16),
        in_specs=[hbm()] * 4,
        out_specs=vmem(),
        scratch_shapes=[
            pltpu.VMEM(ids.shape, ids.dtype),
            pltpu.VMEM(gates.shape, gates.dtype),
            pltpu.VMEM(tokens.shape, tokens.dtype),
            pltpu.VMEM(cotangent.shape, cotangent.dtype),
            pltpu.SemaphoreType.DMA((4,)),
        ],
        compiler_params=params(),
        name="gather_rows",
    )(in_hbm(ids), in_hbm(gates), in_hbm(tokens), in_hbm(cotangent))
    near = exchange(send, orders[0])
    far = swap(near)
    share = near[:, :, width:]
    turned = [
        lax.ppermute(share, "row", [((i + k) % groups, i) for i in range(groups)])
        for k in range(1, groups)
    ]
    square = pltpu.VMEM((sources * TILE, sources * TILE), BF16)
    wide = jax.ShapeDtypeStruct((2 * half, depth), BF16)
    tall = jax.ShapeDtypeStruct((hidden, 2 * half), BF16)
    w_in, x_near, c_near, unfolding, folding = pl.pallas_call(
        functools.partial(near_kernel, tuple(orders[0].index(r) for r in orders[1])),
        out_shape=(
            pltpu.VMEM(w_in.shape, BF16), pltpu.VMEM((half, depth), BF16),
            pltpu.VMEM((half, depth // groups), BF16), square, square,
        ),
        in_specs=[vmem(), hbm()],
        out_specs=[vmem()] * 5,
        scratch_shapes=[pltpu.SemaphoreType.DMA],
        compiler_params=params(),
        cost_estimate=cost(0, 4 * w_in.size),
        name="near_rows",
    )(near, w_in)
    slope = pltpu.VMEM(tall.shape, F32)
    x, hid, gate_slope, up_slope, w_down = pl.pallas_call(
        forward_kernel,
        out_shape=(wide, tall, slope, slope, pltpu.VMEM(w_down.shape, BF16)),
        in_specs=[vmem()] * 4 + [hbm()],
        out_specs=[vmem()] * 5,
        scratch_shapes=[pltpu.SemaphoreType.DMA],
        compiler_params=params(),
        name="gate_up",
    )(far, x_near, unfolding, w_in, w_down)
    hid, turned = lax.optimization_barrier((hid, turned))
    others = [other for array in turned for other in (array, swap(array))]
    halves = (pltpu.VMEM((half, depth), F32), pltpu.VMEM((half, depth), BF16))
    passes = 4 * hidden * depth * half
    keep_out, away_out = pl.pallas_call(
        down_kernel,
        out_shape=halves,
        in_specs=[vmem()] * 2,
        out_specs=[vmem()] * 2,
        compiler_params=params(),
        name="down",
    )(hid, w_down)
    other_out = swap(away_out)
    c, gg, ug = pl.pallas_call(
        functools.partial(hidden_kernel, groups),
        out_shape=(wide, tall, tall),
        in_specs=[vmem()] * (6 + len(others)),
        out_specs=[vmem()] * 3,
        compiler_params=params(),
        cost_estimate=cost(passes, 2 * w_down.size),
        name="hidden_grad",
    )(*others, far, c_near, unfolding, w_down, gate_slope, up_slope)
    keep_grad, away_grad = pl.pallas_call(
        back_kernel,
        out_shape=halves,
        in_specs=[vmem()] * 3,
        out_specs=[vmem()] * 2,
        compiler_params=params(),
        cost_estimate=cost(2 * passes, 2 * w_in.size),
        name="input_grad",
    )(gg, ug, w_in)
    other_grad = swap(away_grad)
    packet = pltpu.HBM((sources, 2 * TILE, width), BF16)
    staging = [pltpu.VMEM((sources, TILE, width), BF16), pltpu.SemaphoreType.DMA((STEPS,))]
    merged = pl.pallas_call(
        merge_first_kernel,
        out_shape=packet,
        in_specs=[vmem()] * 3,
        out_specs=hbm(),
        scratch_shapes=staging,
        compiler_params=params(),
        cost_estimate=cost(0, 8 * half * depth),
        name="merge_out",
    )(folding, keep_out, other_out)
    merged = pl.pallas_call(
        merge_second_kernel,
        out_shape=packet,
        in_specs=[vmem()] * 3 + [hbm()],
        out_specs=hbm(),
        scratch_shapes=staging,
        input_output_aliases={3: 0},
        compiler_params=params(),
        name="merge_grad",
    )(folding, keep_grad, other_grad, merged)
    back = exchange(merged, orders[1])
    grad_in, grad_down = pl.pallas_call(
        weight_kernel,
        grid=(CHUNKS,),
        out_shape=(
            jax.ShapeDtypeStruct((2, hidden, depth), BF16),
            jax.ShapeDtypeStruct((hidden, depth), BF16),
        ),
        in_specs=[pl.BlockSpec((2 * half, width), lambda i: (0, i))] * 2
        + [pl.BlockSpec((hidden, 2 * half), lambda i: (0, 0))] * 3,
        out_specs=(
            pl.BlockSpec((2, hidden, width), lambda i: (0, 0, i)),
            pl.BlockSpec((hidden, width), lambda i: (0, i)),
        ),
        compiler_params=params(),
        cost_estimate=cost(3 * passes, 6 * hidden * depth + 8 * half * depth),
        name="weight_grads",
    )(x, c, hid, gg, ug)
    table = pltpu.VMEM((CHUNKS * rows, experts * TILE), BF16)
    pick, weigh = pl.pallas_call(
        table_kernel,
        out_shape=(table, table),
        in_specs=[vmem(), vmem(), pl.BlockSpec(memory_space=pl.ANY)],
        out_specs=[vmem()] * 2,
        compiler_params=params(),
        name="slot_tables",
    )(ids, gates, gg)
    moe_out, token_grad = pl.pallas_call(
        functools.partial(combine_kernel, places),
        out_shape=(pltpu.HBM((rows, depth), BF16),) * 2,
        in_specs=[vmem()] * 3,
        out_specs=[hbm()] * 2,
        scratch_shapes=[pltpu.VMEM((rows, depth), BF16)] * 2
        + [pltpu.SemaphoreType.DMA((2 * STEPS,))],
        compiler_params=params(),
        name="combine_rows",
    )(back, pick, weigh)
    return (moe_out, token_grad, grad_in[None], grad_down[None])


def solution(mesh):
    tok, exp = mesh.shape["tok"], mesh.shape["exp"]
    fine = Mesh(mesh.devices.reshape(tok // PAIR, PAIR, exp), ("row", "pair", "exp"))
    rows = P(("row", "pair", "exp"), None)
    win, wdown = P("exp", None, ("row", "pair"), None), P("exp", ("row", "pair"), None)
    return jax.shard_map(
        body,
        mesh=fine,
        in_specs=(rows, rows, rows, rows, win, wdown),
        out_specs=(rows, rows, win, wdown),
        check_vma=False,
    )
```

```python
import functools

import jax
import jax.numpy as jnp
import numpy as np
from jax import lax
from jax.experimental import pallas as pl
from jax.experimental.pallas import tpu as pltpu
from jax.sharding import Mesh, PartitionSpec as P

CAP = 2
TILE = 16
CHUNKS = TILE // CAP
PAIR = 2
STEPS = 2
SEEDS = (40, 38)
F32 = jnp.float32
BF16 = jnp.bfloat16
LIMIT = 24 * 1024 * 1024


def iota(shape, dim):
    return lax.broadcasted_iota(jnp.int32, shape, dim)


def dot(a, b, dims=((1,), (0,))):
    return lax.dot_general(a, b, (dims, ((), ())), preferred_element_type=F32)


def vmem():
    return pl.BlockSpec(memory_space=pltpu.VMEM)


def hbm():
    return pl.BlockSpec(memory_space=pltpu.HBM)


def in_hbm(array):
    return pltpu.with_memory_space_constraint(array, pltpu.HBM)


def params():
    return pltpu.CompilerParams(vmem_limit_bytes=LIMIT)


def cost(flops, moved):
    return pl.CostEstimate(flops=flops, bytes_accessed=moved, transcendentals=0)


def slot_tables(ids, gates, experts):
    top, rows = ids.shape
    gates = gates.astype(F32)
    owner = iota((experts, rows), 0)
    member = jnp.zeros((experts, rows), F32)
    gate = jnp.zeros((experts, rows), F32)
    for k in range(top):
        hit = ids[k : k + 1, :] == owner
        member = member + jnp.where(hit, 1.0, 0.0)
        gate = gate + jnp.where(hit, gates[k : k + 1, :], 0.0)
    earlier = jnp.where(iota((rows, rows), 0) < iota((rows, rows), 1), 1.0, 0.0)
    slot = dot(member.astype(BF16), earlier.astype(BF16))
    picks = jnp.concatenate([jnp.where(slot == c, member, 0.0) for c in range(CAP)], axis=0)
    weights = jnp.concatenate([jnp.where(slot == c, gate, 0.0) for c in range(CAP)], axis=0)
    return picks.astype(BF16), weights.astype(BF16)


def message_masks(experts, rows):
    total = experts * TILE
    line = iota((total, CAP * experts), 0)
    spread = iota((total, CAP * experts), 1) == (line % CAP) * experts + line // TILE
    repeat = iota((rows, CHUNKS * rows), 1) % rows == iota((rows, CHUNKS * rows), 0)
    shape = (total, CHUNKS * rows)
    chunk = (iota(shape, 0) // CAP) % CHUNKS == iota(shape, 1) // rows
    return jnp.where(spread, 1.0, 0.0).astype(BF16), jnp.where(repeat, 1.0, 0.0).astype(BF16), chunk


def widen(table, masks):
    spread, repeat, chunk = masks
    small = dot(spread, table).astype(BF16)
    return jnp.where(chunk, dot(small, repeat), 0.0).astype(BF16)


def folded(ref, low, width):
    return jnp.concatenate(
        [ref[:, low + c * width : low + (c + 1) * width] for c in range(CHUNKS)], axis=0
    )


def gather_kernel(
    order, experts, ids_hbm, gates_hbm, tok_hbm, cot_hbm,
    send_ref,
    ids_ref, gates_ref, tok_ref, cot_ref, sems,
):
    rows, depth = tok_ref.shape
    width = depth // CHUNKS
    groups = len(order) // experts
    narrow = width // groups
    pairs = ((ids_hbm, ids_ref), (gates_hbm, gates_ref), (tok_hbm, tok_ref), (cot_hbm, cot_ref))
    copies = [pltpu.make_async_copy(a, b, sems.at[i]) for i, (a, b) in enumerate(pairs)]
    for copy in copies:
        copy.start()
    masks = message_masks(experts, rows)
    copies[0].wait()
    copies[1].wait()
    tables = slot_tables(ids_ref[...], gates_ref[...], experts)
    picks, weights = [widen(table, masks) for table in tables]
    shape = (experts, TILE, -1)
    copies[2].wait()
    moved = dot(picks, folded(tok_ref, 0, width)).astype(BF16).reshape(shape)
    for place, r in enumerate(order):
        send_ref[place, :, 0:width] = moved[r % experts]
    copies[3].wait()
    for g in range(groups):
        moved = dot(weights, folded(cot_ref, g * depth // groups, narrow)).astype(BF16).reshape(shape)
        for place, r in enumerate(order):
            if r // experts == g:
                send_ref[place, :, width : width + narrow] = moved[r % experts]


def table_kernel(ids_ref, gates_ref, after_ref, pick_ref, weigh_ref):
    del after_ref
    rows = ids_ref.shape[1]
    experts = pick_ref.shape[1] // TILE
    masks = message_masks(experts, rows)
    picks, weights = slot_tables(ids_ref[...], gates_ref[...], experts)
    pick_ref[...] = widen(picks, masks).T
    weigh_ref[...] = widen(weights, masks).T


def unfold(messages, perm, out):
    sources, _, width = messages.shape
    half = sources * CAP
    flat = dot(perm, messages.reshape(sources * TILE, width)).astype(BF16)
    for c in range(CHUNKS):
        out[:, c * width : (c + 1) * width] = flat[c * half : (c + 1) * half]


def near_kernel(origins, near_ref, w_in_hbm, w_in_ref, x_ref, c_ref, unfold_ref, fold_ref, sem):
    fetch = pltpu.make_async_copy(w_in_hbm, w_in_ref, sem)
    fetch.start()
    sources = near_ref.shape[0]
    width = x_ref.shape[1] // CHUNKS
    half, lines = sources * CAP, sources * TILE
    row, col = iota((lines, lines), 0), iota((lines, lines), 1)
    perm = (row % half // CAP) * TILE + (row // half) * CAP + row % CAP == col
    perm = jnp.where(perm, 1.0, 0.0).astype(BF16)
    unfold_ref[...] = perm
    unfold(near_ref[:, :, 0:width], perm, x_ref)
    unfold(near_ref[:, :, width:], perm, c_ref)
    row, col = iota((TILE, lines), 0), iota((TILE, lines), 1)
    place = row // CAP * half + row % CAP
    for p, s in enumerate(origins):
        tile = jnp.where(place + s * CAP == col, 1.0, 0.0).astype(BF16)
        fold_ref[p * TILE : (p + 1) * TILE, :] = tile
    fetch.wait()


def forward_kernel(
    far_ref, x_near, unfold_ref, w_in_ref, w_down_hbm,
    x_ref, hid_ref, gate_slope_ref, up_slope_ref, w_down_ref, sem,
):
    fetch = pltpu.make_async_copy(w_down_hbm, w_down_ref, sem)
    fetch.start()
    hidden = w_down_ref.shape[0]
    half = far_ref.shape[0] * CAP
    x_ref[0:half, :] = x_near[...]
    width = x_ref.shape[1] // CHUNKS
    unfold(far_ref[:, :, 0:width], unfold_ref[...], x_ref.at[half : 2 * half])
    both = dot(w_in_ref[...].reshape(2 * hidden, -1), x_ref[...], ((1,), (1,)))
    gate, up = both[:hidden], both[hidden:]
    sig = jax.nn.sigmoid(gate)
    silu = gate * sig
    hid_ref[...] = (silu * up).astype(BF16)
    gate_slope_ref[...] = up * sig * (1.0 + gate * (1.0 - sig))
    up_slope_ref[...] = silu
    fetch.wait()


def split_rows(value, cols, keep_ref, away_ref):
    half = keep_ref.shape[0]
    keep_ref[:, cols] = value[:half]
    away_ref[:, cols] = value[half:].astype(BF16)


def down_kernel(hid_ref, w_down_ref, keep_ref, away_ref):
    width = w_down_ref.shape[1] // CHUNKS
    rows = hid_ref[...].T
    for c in range(CHUNKS):
        cols = pl.ds(c * width, width)
        split_rows(dot(rows, w_down_ref[:, cols]), cols, keep_ref, away_ref)


def hidden_kernel(groups, *refs):
    others, refs = refs[: 2 * (groups - 1)], refs[2 * (groups - 1) :]
    far_ref, c_near, unfold_ref, w_down_ref, gate_slope_ref, up_slope_ref, c_ref, gg_ref, ug_ref = refs
    half, share = c_near.shape
    width = c_ref.shape[1] // CHUNKS
    narrow = share // CHUNKS
    near_rows, far_rows = c_ref.at[0:half], c_ref.at[half : 2 * half]
    plane = lax.axis_index("row")
    bases = [pl.multiple_of(lax.rem(plane + k, groups) * share, share) for k in range(groups)]
    near_rows[:, pl.ds(bases[0], share)] = c_near[...]
    homes = [(far_rows, bases[0])]
    for base in bases[1:]:
        homes += [(near_rows, base), (far_rows, base)]
    lines = unfold_ref.shape[0]
    messages = [far_ref[:, :, width:]] + [other[...] for other in others]
    flat = jnp.concatenate([m.reshape(lines, narrow) for m in messages], axis=1)
    flat = dot(unfold_ref[...], flat).astype(BF16)
    for i, (rows, base) in enumerate(homes):
        for c in range(CHUNKS):
            rows[:, pl.ds(base + c * narrow, narrow)] = flat[
                c * half : (c + 1) * half, i * narrow : (i + 1) * narrow
            ]
    grad = dot(w_down_ref[...], c_ref[...], ((1,), (1,)))
    gg_ref[...] = (grad * gate_slope_ref[...]).astype(BF16)
    ug_ref[...] = (grad * up_slope_ref[...]).astype(BF16)


def back_kernel(gg_ref, ug_ref, w_in_ref, keep_ref, away_ref):
    width = w_in_ref.shape[2] // CHUNKS
    gate_rows, up_rows = gg_ref[...].T, ug_ref[...].T
    for c in range(CHUNKS):
        cols = pl.ds(c * width, width)
        value = dot(gate_rows, w_in_ref[0, :, cols]) + dot(up_rows, w_in_ref[1, :, cols])
        split_rows(value, cols, keep_ref, away_ref)


def merge_rows(part, fold_ref, keep_ref, other_ref, send_hbm, send_ref, sems):
    sources, _, width = send_ref.shape
    pieces = []
    for c in range(CHUNKS):
        cols = pl.ds(c * width, width)
        pieces.append((keep_ref[:, cols] + other_ref[:, cols].astype(F32)).astype(BF16))
    flat = jnp.concatenate(pieces, axis=0)
    each = sources // STEPS
    copies = []
    for step in range(STEPS):
        here = pl.ds(step * each, each)
        rows = dot(fold_ref[step * each * TILE : (step + 1) * each * TILE, :], flat).astype(BF16)
        send_ref[here] = rows.reshape(each, TILE, width)
        copies.append(
            pltpu.make_async_copy(
                send_ref.at[here], send_hbm.at[here, part * TILE : (part + 1) * TILE, :], sems.at[step]
            )
        )
        copies[-1].start()
    for copy in copies:
        copy.wait()


def merge_first_kernel(fold_ref, keep_ref, other_ref, send_hbm, send_ref, sems):
    merge_rows(0, fold_ref, keep_ref, other_ref, send_hbm, send_ref, sems)


def merge_second_kernel(fold_ref, keep_ref, other_ref, first_hbm, send_hbm, send_ref, sems):
    del first_hbm
    merge_rows(1, fold_ref, keep_ref, other_ref, send_hbm, send_ref, sems)


def weight_kernel(x_ref, c_ref, hid_ref, gg_ref, ug_ref, win_ref, wdown_ref):
    x = x_ref[...]
    win_ref[0] = dot(gg_ref[...], x).astype(BF16)
    win_ref[1] = dot(ug_ref[...], x).astype(BF16)
    wdown_ref[...] = dot(hid_ref[...], c_ref[...]).astype(BF16)


def combine_kernel(places, back_ref, pick_ref, weigh_ref, moe_hbm, grad_hbm, moe_ref, grad_ref, sems):
    width = back_ref.shape[2]
    rows = moe_ref.shape[0]
    reach = CHUNKS // STEPS
    copies = []
    for part, (table, out, home) in enumerate(
        ((weigh_ref, moe_ref, moe_hbm), (pick_ref, grad_ref, grad_hbm))
    ):
        lines = slice(part * TILE, (part + 1) * TILE)
        sums = []
        for spots in places:
            total = back_ref[spots[0], lines, :].astype(F32)
            for spot in spots[1:]:
                total = total + back_ref[spot, lines, :].astype(F32)
            sums.append(total.astype(BF16))
        flat = jnp.concatenate(sums, axis=0)
        for step in range(STEPS):
            low = step * reach
            wide = dot(table[low * rows : (low + reach) * rows, :], flat).astype(BF16)
            for c in range(reach):
                out[:, (low + c) * width : (low + c + 1) * width] = wide[c * rows : (c + 1) * rows]
            cols = pl.ds(low * width, reach * width)
            copies.append(pltpu.make_async_copy(out.at[:, cols], home.at[:, cols], sems.at[len(copies)]))
            copies[-1].start()
    for copy in copies:
        copy.wait()


def body(tokens, cotangent, expert_ids, gate_weights, w_in, w_down):
    groups, experts = lax.axis_size("row"), lax.axis_size("exp")
    rows, depth = tokens.shape
    width = depth // CHUNKS
    sources = groups * experts
    half = sources * CAP
    hidden = w_down.shape[1]
    w_in, w_down = in_hbm(w_in[0]), in_hbm(w_down[0])
    ids, gates = expert_ids.T, gate_weights.T
    orders = [[int(r) for r in np.random.RandomState(seed).permutation(sources)] for seed in SEEDS]
    places = tuple(
        tuple(orders[1].index(g * experts + e) for g in range(groups)) for e in range(experts)
    )

    def exchange(array, order):
        planes = [
            [(r // experts * PAIR + p) * experts + r % experts for r in order] for p in range(PAIR)
        ]
        return lax.all_to_all(
            array, ("row", "pair", "exp"), split_axis=0, concat_axis=0, tiled=True,
            axis_index_groups=planes,
        )

    def swap(array):
        return lax.ppermute(array, "pair", [(i, PAIR - 1 - i) for i in range(PAIR)])

    send = pl.pallas_call(
        functools.partial(gather_kernel, orders[0], experts),
        out_shape=pltpu.VMEM((sources, TILE, width + width // groups), BF16),
        in_specs=[hbm()] * 4,
        out_specs=vmem(),
        scratch_shapes=[
            pltpu.VMEM(ids.shape, ids.dtype),
            pltpu.VMEM(gates.shape, gates.dtype),
            pltpu.VMEM(tokens.shape, tokens.dtype),
            pltpu.VMEM(cotangent.shape, cotangent.dtype),
            pltpu.SemaphoreType.DMA((4,)),
        ],
        compiler_params=params(),
        name="gather_rows",
    )(in_hbm(ids), in_hbm(gates), in_hbm(tokens), in_hbm(cotangent))
    near = exchange(send, orders[0])
    far = swap(near)
    share = near[:, :, width:]
    turned = [
        lax.ppermute(share, "row", [((i + k) % groups, i) for i in range(groups)])
        for k in range(1, groups)
    ]
    square = pltpu.VMEM((sources * TILE, sources * TILE), BF16)
    wide = jax.ShapeDtypeStruct((2 * half, depth), BF16)
    tall = jax.ShapeDtypeStruct((hidden, 2 * half), BF16)
    w_in, x_near, c_near, unfolding, folding = pl.pallas_call(
        functools.partial(near_kernel, tuple(orders[0].index(r) for r in orders[1])),
        out_shape=(
            pltpu.VMEM(w_in.shape, BF16), pltpu.VMEM((half, depth), BF16),
            pltpu.VMEM((half, depth // groups), BF16), square, square,
        ),
        in_specs=[vmem(), hbm()],
        out_specs=[vmem()] * 5,
        scratch_shapes=[pltpu.SemaphoreType.DMA],
        compiler_params=params(),
        cost_estimate=cost(0, 4 * w_in.size),
        name="near_rows",
    )(near, w_in)
    slope = pltpu.VMEM(tall.shape, F32)
    x, hid, gate_slope, up_slope, w_down = pl.pallas_call(
        forward_kernel,
        out_shape=(wide, tall, slope, slope, pltpu.VMEM(w_down.shape, BF16)),
        in_specs=[vmem()] * 4 + [hbm()],
        out_specs=[vmem()] * 5,
        scratch_shapes=[pltpu.SemaphoreType.DMA],
        compiler_params=params(),
        name="gate_up",
    )(far, x_near, unfolding, w_in, w_down)
    hid, turned = lax.optimization_barrier((hid, turned))
    others = [other for array in turned for other in (array, swap(array))]
    halves = (pltpu.VMEM((half, depth), F32), pltpu.VMEM((half, depth), BF16))
    passes = 4 * hidden * depth * half
    keep_out, away_out = pl.pallas_call(
        down_kernel,
        out_shape=halves,
        in_specs=[vmem()] * 2,
        out_specs=[vmem()] * 2,
        compiler_params=params(),
        name="down",
    )(hid, w_down)
    other_out = swap(away_out)
    c, gg, ug = pl.pallas_call(
        functools.partial(hidden_kernel, groups),
        out_shape=(wide, tall, tall),
        in_specs=[vmem()] * (6 + len(others)),
        out_specs=[vmem()] * 3,
        compiler_params=params(),
        cost_estimate=cost(passes, 2 * w_down.size),
        name="hidden_grad",
    )(*others, far, c_near, unfolding, w_down, gate_slope, up_slope)
    keep_grad, away_grad = pl.pallas_call(
        back_kernel,
        out_shape=halves,
        in_specs=[vmem()] * 3,
        out_specs=[vmem()] * 2,
        compiler_params=params(),
        cost_estimate=cost(2 * passes, 2 * w_in.size),
        name="input_grad",
    )(gg, ug, w_in)
    other_grad = swap(away_grad)
    packet = pltpu.HBM((sources, 2 * TILE, width), BF16)
    staging = [pltpu.VMEM((sources, TILE, width), BF16), pltpu.SemaphoreType.DMA((STEPS,))]
    merged = pl.pallas_call(
        merge_first_kernel,
        out_shape=packet,
        in_specs=[vmem()] * 3,
        out_specs=hbm(),
        scratch_shapes=staging,
        compiler_params=params(),
        cost_estimate=cost(0, 8 * half * depth),
        name="merge_out",
    )(folding, keep_out, other_out)
    merged = pl.pallas_call(
        merge_second_kernel,
        out_shape=packet,
        in_specs=[vmem()] * 3 + [hbm()],
        out_specs=hbm(),
        scratch_shapes=staging,
        input_output_aliases={3: 0},
        compiler_params=params(),
        name="merge_grad",
    )(folding, keep_grad, other_grad, merged)
    back = exchange(merged, orders[1])
    grad_in, grad_down = pl.pallas_call(
        weight_kernel,
        grid=(CHUNKS,),
        out_shape=(
            jax.ShapeDtypeStruct((2, hidden, depth), BF16),
            jax.ShapeDtypeStruct((hidden, depth), BF16),
        ),
        in_specs=[pl.BlockSpec((2 * half, width), lambda i: (0, i))] * 2
        + [pl.BlockSpec((hidden, 2 * half), lambda i: (0, 0))] * 3,
        out_specs=(
            pl.BlockSpec((2, hidden, width), lambda i: (0, 0, i)),
            pl.BlockSpec((hidden, width), lambda i: (0, i)),
        ),
        compiler_params=params(),
        cost_estimate=cost(3 * passes, 6 * hidden * depth + 8 * half * depth),
        name="weight_grads",
    )(x, c, hid, gg, ug)
    table = pltpu.VMEM((CHUNKS * rows, experts * TILE), BF16)
    pick, weigh = pl.pallas_call(
        table_kernel,
        out_shape=(table, table),
        in_specs=[vmem(), vmem(), pl.BlockSpec(memory_space=pl.ANY)],
        out_specs=[vmem()] * 2,
        compiler_params=params(),
        name="slot_tables",
    )(ids, gates, gg)
    moe_out, token_grad = pl.pallas_call(
        functools.partial(combine_kernel, places),
        out_shape=(pltpu.HBM((rows, depth), BF16),) * 2,
        in_specs=[vmem()] * 3,
        out_specs=[hbm()] * 2,
        scratch_shapes=[pltpu.VMEM((rows, depth), BF16)] * 2
        + [pltpu.SemaphoreType.DMA((2 * STEPS,))],
        compiler_params=params(),
        name="combine_rows",
    )(back, pick, weigh)
    return (moe_out, token_grad, grad_in[None], grad_down[None])


def solution(mesh):
    tok, exp = mesh.shape["tok"], mesh.shape["exp"]
    fine = Mesh(mesh.devices.reshape(tok // PAIR, PAIR, exp), ("row", "pair", "exp"))
    rows = P(("row", "pair", "exp"), None)
    win, wdown = P("exp", None, ("row", "pair"), None), P("exp", ("row", "pair"), None)
    return jax.shard_map(
        body,
        mesh=fine,
        in_specs=(rows, rows, rows, rows, win, wdown),
        out_specs=(rows, rows, win, wdown),
        check_vma=False,
    )
```
